128 devices in a mesh: dp: 8 (over y, core), ctx: 16 (over z, x).
Axes of the slice: x: 4, y: 4, z: 4, core: 2. Of those that a mesh axis runs over, the one named last changes fastest.
Arguments:
- queries: bfloat16 [8, 16, 128, 4096], P('dp', None, 'ctx'), may hold values from -64 to 64
- key_rows: bfloat16 [8, 16, 128, 512], P('dp', None, 'ctx'), may hold values from -24 to 24
- values: bfloat16 [8, 16, 128, 512], P('dp', None, 'ctx'), may hold values from -6 to 6
- out_grad: bfloat16 [8, 16, 128, 4096], P('dp', None, 'ctx'), may hold values from -6 to 6
- out_gain: bfloat16 [4096], replicated, may hold values from 0.099609375 to 1.8984375
- documents: int32 [8, 2048], P('dp'), may hold values from 0 to 63, never falling along the last dimension, each value on 1 to 128 neighbouring positions
Outputs:
- attended: bfloat16 [8, 16, 128, 4096], P('dp', None, 'ctx')
- query_grad: bfloat16 [8, 16, 128, 4096], P('dp', None, 'ctx')
- key_grad: bfloat16 [8, 16, 128, 512], P('dp', None, 'ctx')
- value_grad: bfloat16 [8, 16, 128, 512], P('dp', None, 'ctx')
- gain_grad: float32 [4096], P('ctx')
The draws below stay inside these ranges and needn't reach their ends.
Inputs may be any that keep to these rules, and one draw needn't show every extreme that they name: `documents`: in each sequence the document numbers never fall, and each document covers 1 to 128 consecutive positions; some document covers exactly 128.
All inputs are finite; a program needn't handle non-finite values.
Results may differ from the reference program's by a relative error of at most 0.011.
Values may be sent and summed in bfloat16 or wider, within the bound.
A program may use at most 128 MiB of HBM per device.

```python
import math
import jax
import jax.numpy as jnp
import numpy as np
from jax import lax

KV_HEADS = 4
HEAD_DIM = 128
GROUP = 8
Q_WIDTH = 4096
KV_WIDTH = 512
TOK_DEV = 128
ROUNDS = 16
SEQ = 2048
BATCH = 8
N_CTX = 16


def shared_rows(key):
    base = jax.random.truncated_normal(jax.random.fold_in(key, 101), -6.0, 6.0, (BATCH, ROUNDS, TOK_DEV, KV_WIDTH), jnp.float32)
    return base


def draw_key_rows(key, part):
    base = shared_rows(key)
    return base.astype(jnp.bfloat16)


def draw_queries(key, part):
    key = jax.random.fold_in(key, 11)
    drawn = jax.random.truncated_normal(key, -6.0, 6.0, (BATCH, ROUNDS, TOK_DEV, Q_WIDTH), jnp.float32)
    return drawn.astype(jnp.bfloat16)


def strengthened(array, stream_key, source, target, shards_of, factor):
    def block_of(axis_at):
        return (jnp.arange(array.shape[axis_at]) // (array.shape[axis_at] // shards_of)).reshape((-1,) + (1,) * (array.ndim - 1 - axis_at))

    near = jax.random.permutation(stream_key, shards_of)[block_of(target)]
    other_side = (block_of(target) + shards_of // 2) % shards_of
    return jnp.where((block_of(source) == near) | (block_of(source) == other_side), factor * array, array)


def levels(stream_key, shape, pieces, smallest, largest):
    loudness = 1.0
    for axis_at, parts in pieces:
        draws = jax.random.uniform(jax.random.fold_in(jax.random.fold_in(stream_key, 6), axis_at), (parts,), jnp.float32, smallest / len(pieces), largest / len(pieces))
        loudness = loudness * jnp.repeat(jnp.exp(draws), shape[axis_at] // parts).reshape((-1,) + (1,) * (len(shape) - 1 - axis_at))
    return loudness


def length_profile(amount, total, most, skew):
    weights = [(1 << 20) // math.isqrt(standing ** skew) + 1 for standing in range(2, amount + 1)]
    spare, holding = total - most - (amount - 1), [1] * (amount - 1)
    while spare > 0:
        candidates = [i for i in range(amount - 1) if holding[i] < most]
        pool, budget = sum([weights[i] for i in candidates]), spare
        for i in candidates:
            more = min(most - holding[i], max(1, budget * weights[i] // pool), spare)
            holding[i] = holding[i] + more
            spare = spare - more
    return np.array([most] + holding)


def uneven(stream_key, number_of, total, bound, slope):
    if number_of == 2:
        one = jax.random.randint(stream_key, (), max(1, total - bound), min(bound, total - 1) + 1)
        return jnp.stack([one, total - one])
    lengths = jnp.asarray(length_profile(number_of, total, bound, slope), jnp.int32)
    pairs = (number_of - 1) // 2
    giver, receiver = lengths[1:1 + 2 * pairs:2], lengths[2:2 + 2 * pairs:2]
    slack = jnp.minimum(giver - 1, bound - receiver)
    moved = jax.random.randint(jax.random.fold_in(stream_key, 1), (pairs,), 0, 1 << 20) % (slack + 1)
    lengths = lengths.at[1:1 + 2 * pairs:2].set(giver - moved).at[2:2 + 2 * pairs:2].set(receiver + moved)
    return lengths[jax.random.permutation(jax.random.fold_in(stream_key, 2), number_of)]


def gaussian(own_key, dims, scale, bound, pieces=(), held_as=jnp.bfloat16):
    drawn = jax.random.normal(own_key, dims, jnp.float32) * scale
    if len(pieces) > 0:
        drawn = levels(own_key, dims, pieces, -0.22, 0.18) * drawn
    return jnp.clip(drawn, min=-bound, max=bound).astype(held_as)


def noise_with(stream_key, shape, scale, limit, pieces, heavy, kind=jnp.bfloat16):
    entries = scale * jax.random.normal(stream_key, shape, jnp.float32)
    if pieces:
        entries = entries * levels(stream_key, shape, pieces, -0.22, 0.18)
    return jnp.clip(strengthened(entries, jax.random.fold_in(stream_key, 3), *heavy), -limit, limit).astype(kind)


def setup_inputs(seed: int = 0) -> dict:
    streams_of = jax.random.split(jax.random.key(seed), 7)
    return {
        "queries": draw_queries(jax.random.fold_in(streams_of[6], 71), 0),
        "key_rows": draw_key_rows(jax.random.fold_in(streams_of[6], 71), 0),
        "values": gaussian(streams_of[2], (BATCH, ROUNDS, TOK_DEV, KV_WIDTH), 1.0, 6.0, ((0, 8), (2, 16))),
        "out_grad": noise_with(streams_of[3], (BATCH, ROUNDS, TOK_DEV, Q_WIDTH), 1.0, 6.0, ((0, 8), (2, 16)), (2, 3, 16, 2.0)),
        "out_gain": jnp.clip(1.0 + 0.18 * jax.random.normal(streams_of[4], (Q_WIDTH,), jnp.float32), 0.099609375, 1.8984375).astype(jnp.bfloat16),
        "documents": jax.vmap(lambda own: jnp.searchsorted(jnp.cumsum(uneven(own, 4 * N_CTX, SEQ, TOK_DEV, 2)), jnp.arange(SEQ), side="right"))(jax.random.split(streams_of[5], BATCH)).reshape((BATCH, SEQ)).astype(jnp.int32),
    }


NEG_BIG = -1e+30

def attend_block(q_grp, dout_grp, k_grp, v_grp, allowed):
    f32 = jnp.float32
    scale = 1.0 / math.sqrt(HEAD_DIM)
    scores = jnp.einsum('rqgd,rwd->rgqw', q_grp.astype(f32), k_grp.astype(f32)) * scale
    scores = jnp.where(allowed[:, None], scores, NEG_BIG)
    top = lax.optimization_barrier(jnp.max(scores, axis=-1, keepdims=True))
    expo = jnp.where(allowed[:, None], jnp.exp(scores - top), 0.0)
    probs = expo / lax.optimization_barrier(jnp.sum(expo, axis=-1, keepdims=True))
    probs_low = probs.astype(jnp.bfloat16)
    attn = jnp.einsum('rgqw,rwd->rqgd', probs_low.astype(f32), v_grp.astype(f32)).astype(jnp.bfloat16)
    delta = lax.optimization_barrier(jnp.sum(dout_grp.astype(f32) * attn.astype(f32), axis=-1))
    prob_grad = jnp.einsum('rqgd,rwd->rgqw', dout_grp.astype(f32), v_grp.astype(f32))
    score_grad = (probs * (prob_grad - jnp.transpose(delta, (0, 2, 1))[..., None])).astype(jnp.bfloat16)
    query_grad = (jnp.einsum('rgqw,rwd->rqgd', score_grad.astype(f32), k_grp.astype(f32)) * scale).astype(jnp.bfloat16)
    key_grad = jnp.einsum('rgqw,rqgd->rwd', score_grad.astype(f32), q_grp.astype(f32)) * scale
    value_grad = jnp.einsum('rgqw,rqgd->rwd', probs_low.astype(f32), dout_grp.astype(f32))
    return (attn, query_grad, key_grad, value_grad)

def attend_window(q_rows, dout_rows, k_win, v_win, allowed):
    rounds, width = (q_rows.shape[0], q_rows.shape[1])
    span = k_win.shape[1]
    q_grp = jnp.moveaxis(q_rows.reshape(rounds, width, KV_HEADS, GROUP, HEAD_DIM), 2, 0)
    d_grp = jnp.moveaxis(dout_rows.reshape(rounds, width, KV_HEADS, GROUP, HEAD_DIM), 2, 0)
    k_grp = jnp.moveaxis(k_win.reshape(rounds, span, KV_HEADS, HEAD_DIM), 2, 0)
    v_grp = jnp.moveaxis(v_win.reshape(rounds, span, KV_HEADS, HEAD_DIM), 2, 0)

    def one_head(items):
        return attend_block(items[0], items[1], items[2], items[3], allowed)
    attn, query_grad, key_grad, value_grad = lax.map(one_head, (q_grp, d_grp, k_grp, v_grp))
    attn = jnp.moveaxis(attn, 0, 2).reshape(rounds, width, Q_WIDTH)
    query_grad = jnp.moveaxis(query_grad, 0, 2).reshape(rounds, width, Q_WIDTH)
    key_grad = jnp.moveaxis(key_grad, 0, 2).reshape(rounds, span, KV_WIDTH)
    value_grad = jnp.moveaxis(value_grad, 0, 2).reshape(rounds, span, KV_WIDTH)
    return (attn, query_grad, key_grad, value_grad)

def reference(queries, key_rows, values, out_grad, out_gain, documents):
    f32 = jnp.float32
    head_grad = (out_gain.astype(f32) * out_grad.astype(f32)).astype(jnp.bfloat16)
    docs = documents.reshape(BATCH, ROUNDS, TOK_DEV).astype(jnp.int32)
    prev_docs = jnp.concatenate([jnp.full((BATCH, 1, TOK_DEV), -1, jnp.int32), docs[:, :-1]], axis=1)
    zero_round = jnp.zeros_like(key_rows[:, :1])
    k_win = jnp.concatenate([jnp.concatenate([zero_round, key_rows[:, :-1]], axis=1), key_rows], axis=2)
    v_win = jnp.concatenate([jnp.concatenate([zero_round, values[:, :-1]], axis=1), values], axis=2)
    doc_win = jnp.concatenate([prev_docs, docs], axis=2)
    column = jnp.arange(TOK_DEV, dtype=jnp.int32)
    later = jnp.concatenate([jnp.ones((TOK_DEV, TOK_DEV), dtype=bool), column[None, :] <= column[:, None]], axis=1)

    def one_sequence(items):
        q_seq, d_seq, k_seq, v_seq, doc_seq, own_seq = items
        allowed = (doc_seq[:, None, :] == own_seq[:, :, None]) & later[None]
        return attend_window(q_seq, d_seq, k_seq, v_seq, allowed)
    attn, query_grad, k_part, v_part = lax.map(one_sequence, (queries, head_grad, k_win, v_win, doc_win, docs))
    tail = jnp.zeros_like(k_part[:, :1, :TOK_DEV])
    key_grad = k_part[:, :, TOK_DEV:] + jnp.concatenate([k_part[:, 1:, :TOK_DEV], tail], axis=1)
    value_grad = v_part[:, :, TOK_DEV:] + jnp.concatenate([v_part[:, 1:, :TOK_DEV], tail], axis=1)
    attended = (out_gain.astype(f32) * attn.astype(f32)).astype(jnp.bfloat16)
    total = lax.optimization_barrier(jnp.sum(out_grad.astype(f32) * attn.astype(f32), axis=(0, 1, 2)))
    gain_grad = total * (1.0 / math.sqrt(BATCH * SEQ))
    return (attended, query_grad, key_grad.astype(jnp.bfloat16), value_grad.astype(jnp.bfloat16), gain_grad)
```

```python
import functools
import math

import jax
import jax.numpy as jnp
from jax import lax
from jax.experimental import pallas as pl
from jax.experimental.pallas import tpu as pltpu
from jax.sharding import PartitionSpec as P

MESH = pl.DeviceIdType.MESH
F32 = jnp.float32
BF16 = jnp.bfloat16
SIDE = 4
ROUNDS = 16
OWN = ROUNDS // SIDE
SLOTS = OWN + 1
WIDE = 8
DIM = 128
GROUP = 8
HEADS = 4
TOK = 128
ROWS = SIDE * WIDE * GROUP
NEG_BIG = -1e30
UNIT_HEAD = (0, 2, 1, 3)


def dot_t(a, b):
    return lax.dot_general(a, b, (((1,), (1,)), ((), ())), preferred_element_type=F32)


def dot_tn(a, b):
    return lax.dot_general(a, b, (((0,), (0,)), ((), ())), preferred_element_type=F32)


def dot_n(a, b):
    return lax.dot_general(a, b, (((1,), (0,)), ((), ())), preferred_element_type=F32)


def kernel(
    q_hbm, k_hbm, v_hbm, g_hbm, gain_ref, docs_ref,
    att_hbm, dq_hbm, dk_ref, dv_ref, gg_ref,
    qin, gin, kin, vin, att_o, dq_o, kp, vp, kr, vr, ks, vs, ka, va,
    le_ref, bias_ref, kacc, vacc, gacc, gsend, grecv, gsum, gdp,
    kv_send, kv_recv, kvg_send, kvg_recv, q_send, q_recv, out_send, out_recv,
    rs_send, rs_recv, aa_send, aa_recv, g_send, g_recv, d_send, d_recv,
):
    dp = lax.axis_index("dp")
    ctx = lax.axis_index("ctx")
    z = ctx // SIDE
    x = ctx % SIDE
    scale = 1.0 / math.sqrt(DIM)

    def at_ctx(c):
        return (dp, c)

    def a_peer(t, k):
        a = ((x if t == 0 else z) + k) % SIDE
        return a, at_ctx(z * SIDE + a if t == 0 else a * SIDE + x)

    def g_peer(t, k):
        g = ((z if t == 0 else x) + k) % SIDE
        return g, at_ctx(g * SIDE + x if t == 0 else z * SIDE + g)

    def me_a(t):
        return x if t == 0 else z

    def me_g(t):
        return z if t == 0 else x

    def off(a):
        return (a + SIDE - 1) // SIDE

    def remote(src, dst, ssem, rsem, dev):
        pltpu.make_async_remote_copy(
            src_ref=src, dst_ref=dst, send_sem=ssem, recv_sem=rsem, device_id=dev, device_id_type=MESH
        ).start()

    def local(src, dst, sem):
        pltpu.make_async_copy(src, dst, sem).start()

    def drain(ref, sem):
        pltpu.make_async_copy(ref, ref, sem).wait()

    barrier = pltpu.get_barrier_semaphore()
    for i in range(1, 16):
        pl.semaphore_signal(barrier, inc=1, device_id=at_ctx((ctx + i) % 16), device_id_type=MESH)
    for i in range(1, 8):
        pl.semaphore_signal(barrier, inc=1, device_id=((dp + i) % 8, ctx), device_id_type=MESH)

    def kv_local(u):
        t, h = u % 2, UNIT_HEAD[u]
        a = me_a(t)
        lanes = pl.ds(h * DIM, DIM)
        for n, (src, dst) in enumerate(((k_hbm, kin), (v_hbm, vin))):
            local(src.at[0, pl.ds(OWN * a - off(a), SLOTS), :, lanes], dst.at[u, me_g(t), a], kv_recv.at[u, n])

    def q_local(u):
        t, h = u % 2, UNIT_HEAD[u]
        a = me_a(t)
        lanes = pl.ds(h * GROUP * DIM, GROUP * DIM)
        for n, (src, dst) in enumerate(((q_hbm, qin), (g_hbm, gin))):
            local(src.at[0, pl.ds(OWN * a, OWN), :, lanes], dst.at[u, a], q_recv.at[u, n])

    def kv_first(u):
        t, h = u % 2, UNIT_HEAD[u]
        lanes = pl.ds(h * DIM, DIM)
        for k in (1, 3, 2):
            a, dev = a_peer(t, k)
            for n, (src, dst) in enumerate(((k_hbm, kin), (v_hbm, vin))):
                remote(
                    src.at[0, pl.ds(OWN * a - off(a), SLOTS), :, lanes], dst.at[u, me_g(t), me_a(t)],
                    kv_send.at[n], kv_recv.at[u, n], dev,
                )

    def kv_gather(u):
        t = u % 2
        for n, buf in enumerate((kin, vin)):
            drain(buf.at[u, 0], kv_recv.at[u, n])
        for k in (1, 3, 2):
            _, dev = g_peer(t, k)
            for n, buf in enumerate((kin, vin)):
                remote(buf.at[u, me_g(t)], buf.at[u, me_g(t)], kvg_send.at[n], kvg_recv.at[u, n], dev)

    def q_send_all(u):
        t, h = u % 2, UNIT_HEAD[u]
        lanes = pl.ds(h * GROUP * DIM, GROUP * DIM)
        for k in (1, 3, 2):
            a, dev = a_peer(t, k)
            for n, (src, dst) in enumerate(((q_hbm, qin), (g_hbm, gin))):
                remote(
                    src.at[0, pl.ds(OWN * a, OWN), :, lanes], dst.at[u, me_a(t)], q_send.at[n], q_recv.at[u, n], dev
                )

    for u in range(4):
        kv_local(u)
    for u in range(4):
        q_local(u)
    pl.semaphore_wait(barrier, 22)
    for u in range(4):
        kv_first(u)
    for u in (0, 1):
        q_send_all(u)
    for u in range(4):
        kv_gather(u)
    for u in (2, 3):
        q_send_all(u)

    key_i = lax.broadcasted_iota(jnp.int32, (TOK, ROWS), 0)
    row_i = lax.broadcasted_iota(jnp.int32, (TOK, ROWS), 1) & (SIDE * WIDE - 1)
    for t in range(2):
        def key_col(i):
            return i if t == 0 else ((i >> 3) & 3) * 32 + (i >> 5) * 8 + (i & 7)

        def row_col(i):
            i = i & (SIDE * WIDE - 1)
            return z * 32 + i if t == 0 else (i >> 3) * 32 + x * 8 + (i & 7)

        le = key_col(key_i) <= row_col(row_i)
        le_ref[t] = jnp.where(le, 1.0, 0.0)
        perm = jnp.where(
            key_col(lax.broadcasted_iota(jnp.int32, (TOK, TOK), 0)) == lax.broadcasted_iota(jnp.int32, (TOK, TOK), 1),
            1.0, 0.0,
        ).astype(BF16)
        sel = jnp.where(
            row_col(lax.broadcasted_iota(jnp.int32, (ROWS, TOK), 0)) == lax.broadcasted_iota(jnp.int32, (ROWS, TOK), 1),
            1.0, 0.0,
        ).astype(BF16)

        def doc_row(r):
            return docs_ref[0:1, pl.ds(pl.multiple_of(r * TOK, TOK), TOK)].astype(F32)

        def one_bias(r, _):
            rho = me_a(t) * OWN + r
            cur = doc_row(rho)
            prev = doc_row((rho + ROUNDS - 1) % ROUNDS)
            k_cur = dot_t(perm, jnp.broadcast_to(cur, (ROWS, TOK)).astype(BF16))
            k_prev = dot_t(perm, jnp.broadcast_to(prev, (ROWS, TOK)).astype(BF16))
            q_doc = dot_t(jnp.broadcast_to(cur, (TOK, TOK)).astype(BF16), sel)
            k_prev = jnp.where(rho > 0, k_prev, -1.0)
            mine = jnp.where(le_ref[t] > 0.5, k_cur, k_prev)
            bias_ref[t, r] = jnp.where(mine == q_doc, 0.0, NEG_BIG)
            return 0

        lax.fori_loop(0, OWN, one_bias, 0)

    def unit(u):
        t, h = u % 2, UNIT_HEAD[u]
        a = me_a(t)
        lanes = pl.ds(h * GROUP * DIM, GROUP * DIM)
        for n, buf in enumerate((qin, gin)):
            drain(buf.at[u], q_recv.at[u, n])
        for n, buf in enumerate((kin, vin)):
            drain(buf.at[u, pl.ds(0, SIDE - 1)], kvg_recv.at[u, n])
        kacc[...] = jnp.zeros_like(kacc)
        vacc[...] = jnp.zeros_like(vacc)
        gacc[...] = jnp.zeros_like(gacc)

        def one_round(r, _):
            here = r + off(a)
            before = (here + SLOTS - 1) % SLOTS

            def keys(buf, s):
                return buf[u, :, :, s].astype(F32).reshape(TOK, DIM)

            k_win = jnp.concatenate([keys(kin, here), keys(kin, before)], axis=0).astype(BF16)
            v_win = jnp.concatenate([keys(vin, here), keys(vin, before)], axis=0).astype(BF16)
            q_rows = jnp.concatenate(
                [qin[u, :, r, :, g * DIM : (g + 1) * DIM].astype(F32).reshape(SIDE * WIDE, DIM) for g in range(GROUP)],
                axis=0,
            ).astype(BF16)
            hg = jnp.concatenate(
                [
                    gin[u, :, r, :, g * DIM : (g + 1) * DIM].astype(F32).reshape(SIDE * WIDE, DIM)
                    * gain_ref[h * GROUP + g : h * GROUP + g + 1, :]
                    for g in range(GROUP)
                ],
                axis=0,
            ).astype(BF16)
            le = le_ref[t] > 0.5
            s_all = dot_t(k_win, q_rows)
            s = jnp.where(le, s_all[:TOK], s_all[TOK:]) * (scale * math.log2(math.e)) + bias_ref[t, r]
            e = jnp.exp2(s - jnp.max(s, axis=0, keepdims=True))
            p = e * (1.0 / jnp.sum(e, axis=0, keepdims=True))
            d_all = dot_t(v_win, hg)
            d = jnp.where(le, d_all[:TOK], d_all[TOK:])
            ds = p * (d - jnp.sum(p * d, axis=0, keepdims=True))
            p2 = jnp.concatenate([jnp.where(le, p, 0.0), jnp.where(le, 0.0, p)], axis=0).astype(BF16)
            ds2 = jnp.concatenate([jnp.where(le, ds, 0.0), jnp.where(le, 0.0, ds)], axis=0).astype(BF16)
            attn = dot_tn(p2, v_win).astype(BF16).astype(F32)
            dq = dot_tn(ds2, k_win) * scale
            dv = dot_n(p2, hg)
            dk = dot_n(ds2, q_rows) * scale
            for g in range(GROUP):
                rows = slice(g * SIDE * WIDE, (g + 1) * SIDE * WIDE)
                cols = slice(g * DIM, (g + 1) * DIM)
                a_g = attn[rows].reshape(SIDE, WIDE, DIM)
                gacc[g] += jnp.sum(a_g * gin[u, :, r, :, cols].astype(F32), axis=0)
                att_o[u, :, r, :, cols] = (a_g * gain_ref[h * GROUP + g : h * GROUP + g + 1, :]).astype(BF16)
                dq_o[u, :, r, :, cols] = dq[rows].reshape(SIDE, WIDE, DIM).astype(BF16)
            kp[u, :, :, before] = (kacc[...] + dk[TOK:]).reshape(SIDE, SIDE, WIDE, DIM).astype(BF16)
            vp[u, :, :, before] = (vacc[...] + dv[TOK:]).reshape(SIDE, SIDE, WIDE, DIM).astype(BF16)
            kacc[...] = dk[:TOK]
            vacc[...] = dv[:TOK]
            for n, (buf, dst) in enumerate(((att_o, att_hbm), (dq_o, dq_hbm))):
                for k in (1, 3, 2):
                    b, dev = a_peer(t, k)
                    remote(
                        buf.at[u, b, r], dst.at[0, OWN * a + r, :, lanes], out_send.at[n], out_recv.at[n], dev
                    )
                local(buf.at[u, a, r], dst.at[0, OWN * a + r, :, lanes], out_recv.at[n])
            return 0

        lax.fori_loop(0, OWN, one_round, 0)
        last = OWN - 1 + off(a)
        kp[u, :, :, last] = kacc[...].reshape(SIDE, SIDE, WIDE, DIM).astype(BF16)
        vp[u, :, :, last] = vacc[...].reshape(SIDE, SIDE, WIDE, DIM).astype(BF16)
        for k in (1, 3, 2):
            g, dev = g_peer(t, k)
            for n, (src, dst) in enumerate(((kp, kr), (vp, vr))):
                remote(src.at[u, g], dst.at[u, k - 1], rs_send.at[n], rs_recv.at[u, n], dev)
        for i in range(SIDE):
            for j in range(2):
                gsend[u, i, j : j + 1, :] = jnp.sum(gacc[2 * i + j], axis=0, keepdims=True)
        for i in range(SIDE):
            owner = h * SIDE + i

            @pl.when(owner != ctx)
            def _():
                remote(gsend.at[u, i], grecv.at[(ctx - owner + 15) % 16], g_send, g_recv, at_ctx(owner))

    def reduce_back(u):
        t = u % 2
        for n, (part, got, total, back) in enumerate(((kp, kr, ks, ka), (vp, vr, vs, va))):
            drain(got.at[u], rs_recv.at[u, n])
            acc = part[u, me_g(t)].astype(F32)
            for k in range(SIDE - 1):
                acc += got[u, k].astype(F32)
            total[u] = acc.astype(BF16)
            for k in (1, 3, 2):
                b, dev = a_peer(t, k)
                remote(total.at[u, b], back.at[u, me_a(t)], aa_send.at[n], aa_recv.at[u, n], dev)
            local(total.at[u, me_a(t)], back.at[u, me_a(t)], aa_recv.at[u, n])

    def finish(u):
        h = UNIT_HEAD[u]
        cols = slice(h * DIM, (h + 1) * DIM)
        for n, (back, out) in enumerate(((ka, dk_ref), (va, dv_ref))):
            drain(back.at[u], aa_recv.at[u, n])
            for rho in range(ROUNDS):
                b, r = rho // OWN, rho % OWN
                val = back[u, b, r if b == 0 else r + 1]
                if r == OWN - 1 and b < SIDE - 1:
                    val = (val.astype(F32) + back[u, b + 1, 0].astype(F32)).astype(BF16)
                out[0, rho, :, cols] = val

    gsend[...] = jnp.zeros_like(gsend)
    for u in range(4):
        unit(u)
        if u >= 1:
            reduce_back(u - 1)
    drain(grecv.at[pl.ds(0, 15)], g_recv)
    total = jnp.zeros((8, DIM), F32)
    for u in range(4):
        for i in range(SIDE):
            total += jnp.where(UNIT_HEAD[u] * SIDE + i == ctx, gsend[u, i], 0.0)
    for i in range(15):
        total += grecv[i]
    gsum[...] = total
    for i in range(1, 8):
        remote(gsum, gdp.at[i - 1], d_send, d_recv, ((dp + i) % 8, ctx))
    reduce_back(3)
    for u in range(3):
        finish(u)
    drain(gdp.at[pl.ds(0, 7)], d_recv)
    total = gsum[...]
    for i in range(7):
        total += gdp[i]
    gg_ref[...] = total[:2] * (1.0 / 128.0)
    finish(3)
    for n, buf in enumerate((kin, vin)):
        drain(buf.at[:, 0, pl.ds(0, SIDE - 1)], kv_send.at[n])
        drain(buf.at[:, pl.ds(0, SIDE - 1)], kvg_send.at[n])
    for n, buf in enumerate((qin, gin)):
        drain(buf.at[:, pl.ds(0, SIDE - 1)], q_send.at[n])
    for n, buf in enumerate((kr, vr)):
        drain(buf, rs_send.at[n])
    for n, buf in enumerate((ka, va)):
        drain(buf.at[:, pl.ds(0, SIDE - 1)], aa_send.at[n])
    for n, (buf, dst) in enumerate(((att_o, att_hbm), (dq_o, dq_hbm))):
        drain(buf.at[:, pl.ds(0, SIDE - 1)], out_send.at[n])
        drain(dst, out_recv.at[n])
    drain(grecv.at[pl.ds(0, 15)], g_send)
    drain(gdp.at[pl.ds(0, 7)], d_send)


def body(queries, key_rows, values, out_grad, out_gain, documents):
    gain = out_gain.reshape(HEADS * GROUP, DIM).astype(F32)
    any_spec = pl.BlockSpec(memory_space=pl.ANY)
    vmem = pl.BlockSpec(memory_space=pltpu.VMEM)
    wide = pltpu.VMEM((4, SIDE, OWN, WIDE, GROUP * DIM), BF16)
    narrow = pltpu.VMEM((4, SIDE, SIDE, SLOTS, WIDE, DIM), BF16)
    narrow3 = pltpu.VMEM((4, SIDE - 1, SIDE, SLOTS, WIDE, DIM), BF16)
    flat = pltpu.VMEM((4, SIDE, SLOTS, WIDE, DIM), BF16)
    dma = pltpu.SemaphoreType.DMA
    att, dq, dk, dv, gg = pl.pallas_call(
        kernel,
        out_shape=(
            jax.ShapeDtypeStruct(queries.shape, BF16),
            jax.ShapeDtypeStruct(queries.shape, BF16),
            jax.ShapeDtypeStruct(key_rows.shape, BF16),
            jax.ShapeDtypeStruct(key_rows.shape, BF16),
            jax.ShapeDtypeStruct((2, DIM), F32),
        ),
        in_specs=[any_spec, any_spec, any_spec, any_spec, vmem, vmem],
        out_specs=(any_spec, any_spec, vmem, vmem, vmem),
        scratch_shapes=[
            wide, wide, narrow, narrow, wide, wide, narrow, narrow, narrow3, narrow3, flat, flat, flat, flat,
            pltpu.VMEM((2, TOK, ROWS), F32),
            pltpu.VMEM((2, OWN, TOK, ROWS), F32),
            pltpu.VMEM((TOK, DIM), F32),
            pltpu.VMEM((TOK, DIM), F32),
            pltpu.VMEM((GROUP, WIDE, DIM), F32),
            pltpu.VMEM((4, SIDE, 8, DIM), F32),
            pltpu.VMEM((15, 8, DIM), F32),
            pltpu.VMEM((8, DIM), F32),
            pltpu.VMEM((7, 8, DIM), F32),
            dma((2,)), dma((4, 2)), dma((2,)), dma((4, 2)), dma((2,)), dma((4, 2)), dma((2,)), dma((2,)),
            dma((2,)), dma((4, 2)), dma((2,)), dma((4, 2)), dma, dma, dma, dma,
        ],
        compiler_params=pltpu.CompilerParams(
            collective_id=0, has_side_effects=True, vmem_limit_bytes=48 * 1024 * 1024
        ),
        name="packed_attention",
    )(queries, key_rows, values, out_grad, gain, documents)
    return att, dq, dk, dv, gg.reshape(2 * DIM)


def solution(mesh):
    tokens = P("dp", None, "ctx", None)
    return jax.shard_map(
        body,
        mesh=mesh,
        in_specs=(tokens, tokens, tokens, tokens, P(), P("dp", None)),
        out_specs=(tokens, tokens, tokens, tokens, P("ctx")),
        check_vma=False,
    )
```

```python
import functools
import math

import jax
import jax.numpy as jnp
from jax import lax
from jax.experimental import pallas as pl
from jax.experimental.pallas import tpu as pltpu
from jax.sharding import PartitionSpec as P

MESH = pl.DeviceIdType.MESH
F32 = jnp.float32
BF16 = jnp.bfloat16
SIDE = 4
ROUNDS = 16
OWN = ROUNDS // SIDE
SLOTS = OWN + 1
WIDE = 8
DIM = 128
GROUP = 8
HEADS = 4
TOK = 128
ROWS = SIDE * WIDE * GROUP
NEG_BIG = -1e30
UNIT_HEAD = (0, 2, 1, 3)


def dot_t(a, b):
    return lax.dot_general(a, b, (((1,), (1,)), ((), ())), preferred_element_type=F32)


def dot_tn(a, b):
    return lax.dot_general(a, b, (((0,), (0,)), ((), ())), preferred_element_type=F32)


def dot_n(a, b):
    return lax.dot_general(a, b, (((1,), (0,)), ((), ())), preferred_element_type=F32)


def kernel(
    q_hbm, k_hbm, v_hbm, g_hbm, gain_hbm, docs_hbm,
    att_hbm, dq_hbm, dk_ref, dv_ref, gg_ref,
    qin, gin, kin, vin, att_o, dq_o, kp, vp, kr, vr, ks, vs, ka, va,
    gain_ref, docs_ref, le_ref, bias_ref, kacc, vacc, gacc, gains, gpart, ghalf, gsum, gside, gfin, gdp,
    kv_send, kv_recv, kvg_send, kvg_recv, q_send, q_recv, out_send, out_recv,
    rs_send, rs_recv, aa_send, aa_recv, gr_send, gr_recv, ga_send, ga_recv, d_send, d_recv, small,
):
    dp = lax.axis_index("dp")
    ctx = lax.axis_index("ctx")
    z = ctx // SIDE
    x = ctx % SIDE
    scale = 1.0 / math.sqrt(DIM)

    def at_ctx(c):
        return (dp, c)

    def a_peer(t, k):
        a = ((x if t == 0 else z) + k) % SIDE
        return a, at_ctx(z * SIDE + a if t == 0 else a * SIDE + x)

    def g_peer(t, k):
        g = ((z if t == 0 else x) + k) % SIDE
        return g, at_ctx(g * SIDE + x if t == 0 else z * SIDE + g)

    def me_a(t):
        return x if t == 0 else z

    def me_g(t):
        return z if t == 0 else x

    def off(a):
        return (a + SIDE - 1) // SIDE

    def remote(src, dst, ssem, rsem, dev):
        pltpu.make_async_remote_copy(
            src_ref=src, dst_ref=dst, send_sem=ssem, recv_sem=rsem, device_id=dev, device_id_type=MESH
        ).start()

    def local(src, dst, sem):
        pltpu.make_async_copy(src, dst, sem).start()

    def drain(ref, sem):
        pltpu.make_async_copy(ref, ref, sem).wait()

    barrier = pltpu.get_barrier_semaphore()
    for t in range(2):
        for k in range(1, SIDE):
            pl.semaphore_signal(barrier, inc=1, device_id=a_peer(t, k)[1], device_id_type=MESH)
    for i in range(1, 8):
        pl.semaphore_signal(barrier, inc=1, device_id=((dp + i) % 8, ctx), device_id_type=MESH)

    def kv_local(u):
        t, h = u % 2, UNIT_HEAD[u]
        a = me_a(t)
        lanes = pl.ds(h * DIM, DIM)
        for n, (src, dst) in enumerate(((k_hbm, kin), (v_hbm, vin))):
            local(src.at[0, pl.ds(OWN * a - off(a), SLOTS), :, lanes], dst.at[u, me_g(t), a], kv_recv.at[u, n])

    def q_local(u):
        t, h = u % 2, UNIT_HEAD[u]
        a = me_a(t)
        lanes = pl.ds(h * GROUP * DIM, GROUP * DIM)
        for n, (src, dst) in enumerate(((q_hbm, qin), (g_hbm, gin))):
            local(src.at[0, pl.ds(OWN * a, OWN), :, lanes], dst.at[u, a], q_recv.at[u, n])

    def kv_first(u):
        t, h = u % 2, UNIT_HEAD[u]
        lanes = pl.ds(h * DIM, DIM)
        for k in (1, 3, 2):
            a, dev = a_peer(t, k)
            for n, (src, dst) in enumerate(((k_hbm, kin), (v_hbm, vin))):
                remote(
                    src.at[0, pl.ds(OWN * a - off(a), SLOTS), :, lanes], dst.at[u, me_g(t), me_a(t)],
                    kv_send.at[n], kv_recv.at[u, n], dev,
                )

    def kv_gather(u):
        t = u % 2
        for n, buf in enumerate((kin, vin)):
            drain(buf.at[u, 0], kv_recv.at[u, n])
        for k in (1, 3, 2):
            _, dev = g_peer(t, k)
            for n, buf in enumerate((kin, vin)):
                remote(buf.at[u, me_g(t)], buf.at[u, me_g(t)], kvg_send.at[n], kvg_recv.at[u, n], dev)

    def q_send_all(u):
        t, h = u % 2, UNIT_HEAD[u]
        lanes = pl.ds(h * GROUP * DIM, GROUP * DIM)
        for k in (1, 3, 2):
            a, dev = a_peer(t, k)
            for n, (src, dst) in enumerate(((q_hbm, qin), (g_hbm, gin))):
                remote(
                    src.at[0, pl.ds(OWN * a, OWN), :, lanes], dst.at[u, me_a(t)], q_send.at[n], q_recv.at[u, n], dev
                )

    local(gain_hbm, gain_ref, small.at[0])
    local(docs_hbm, docs_ref, small.at[1])
    for u in range(4):
        kv_local(u)
    for u in range(4):
        q_local(u)
    pl.semaphore_wait(barrier, 13)
    for u in range(4):
        kv_first(u)
    for u in (0, 1):
        q_send_all(u)
    for u in range(4):
        kv_gather(u)
    for u in (2, 3):
        q_send_all(u)

    drain(gain_ref, small.at[0])
    drain(docs_ref, small.at[1])
    for i in range(HEADS * GROUP):
        gains[i : i + 1, :] = gain_ref[pl.ds(i * DIM, DIM)].astype(F32).reshape(1, DIM)
    key_i = lax.broadcasted_iota(jnp.int32, (TOK, ROWS), 0)
    row_i = lax.broadcasted_iota(jnp.int32, (TOK, ROWS), 1) & (SIDE * WIDE - 1)
    for t in range(2):
        def key_col(i):
            return i if t == 0 else ((i >> 3) & 3) * 32 + (i >> 5) * 8 + (i & 7)

        def row_col(i):
            i = i & (SIDE * WIDE - 1)
            return z * 32 + i if t == 0 else (i >> 3) * 32 + x * 8 + (i & 7)

        le = key_col(key_i) <= row_col(row_i)
        le_ref[t] = jnp.where(le, 1.0, 0.0)
        perm = jnp.where(
            key_col(lax.broadcasted_iota(jnp.int32, (TOK, TOK), 0)) == lax.broadcasted_iota(jnp.int32, (TOK, TOK), 1),
            1.0, 0.0,
        ).astype(BF16)
        sel = jnp.where(
            row_col(lax.broadcasted_iota(jnp.int32, (ROWS, TOK), 0)) == lax.broadcasted_iota(jnp.int32, (ROWS, TOK), 1),
            1.0, 0.0,
        ).astype(BF16)

        def doc_row(r):
            return docs_ref[0:1, pl.ds(pl.multiple_of(r * TOK, TOK), TOK)].astype(F32)

        def one_bias(r, _):
            rho = me_a(t) * OWN + r
            cur = doc_row(rho)
            prev = doc_row((rho + ROUNDS - 1) % ROUNDS)
            k_cur = dot_t(perm, jnp.broadcast_to(cur, (ROWS, TOK)).astype(BF16))
            k_prev = dot_t(perm, jnp.broadcast_to(prev, (ROWS, TOK)).astype(BF16))
            q_doc = dot_t(jnp.broadcast_to(cur, (TOK, TOK)).astype(BF16), sel)
            k_prev = jnp.where(rho > 0, k_prev, -1.0)
            mine = jnp.where(le_ref[t] > 0.5, k_cur, k_prev)
            bias_ref[t, r] = jnp.where(mine == q_doc, 0.0, NEG_BIG)
            return 0

        lax.fori_loop(0, OWN, one_bias, 0)

    def bulk(u, r, count):
        t, h = u % 2, UNIT_HEAD[u]
        a = me_a(t)
        lanes = pl.ds(h * GROUP * DIM, GROUP * DIM)
        rounds = pl.ds(r, count)
        for n, (buf, dst) in enumerate(((att_o, att_hbm), (dq_o, dq_hbm))):
            there = dst.at[0, pl.ds(OWN * a + r, count), :, lanes]
            for k in (1, 3, 2):
                b, dev = a_peer(t, k)
                remote(buf.at[u, b, rounds], there, out_send.at[n], out_recv.at[n], dev)
            local(buf.at[u, a, rounds], there, out_recv.at[n])

    def unit(u):
        t, h = u % 2, UNIT_HEAD[u]
        a = me_a(t)
        for n, buf in enumerate((qin, gin)):
            drain(buf.at[u], q_recv.at[u, n])
        for n, buf in enumerate((kin, vin)):
            drain(buf.at[u, pl.ds(0, SIDE - 1)], kvg_recv.at[u, n])
        kacc[...] = jnp.zeros_like(kacc)
        vacc[...] = jnp.zeros_like(vacc)
        gacc[...] = jnp.zeros_like(gacc)

        def one_round(r, _):
            here = r + off(a)
            before = (here + SLOTS - 1) % SLOTS

            def keys(buf, s):
                return buf[u, :, :, s].astype(F32).reshape(TOK, DIM)

            k_win = jnp.concatenate([keys(kin, here), keys(kin, before)], axis=0).astype(BF16)
            v_win = jnp.concatenate([keys(vin, here), keys(vin, before)], axis=0).astype(BF16)
            q_rows = jnp.concatenate(
                [qin[u, :, r, :, g * DIM : (g + 1) * DIM].astype(F32).reshape(SIDE * WIDE, DIM) for g in range(GROUP)],
                axis=0,
            ).astype(BF16)
            hg = jnp.concatenate(
                [
                    gin[u, :, r, :, g * DIM : (g + 1) * DIM].astype(F32).reshape(SIDE * WIDE, DIM)
                    * gains[h * GROUP + g : h * GROUP + g + 1, :]
                    for g in range(GROUP)
                ],
                axis=0,
            ).astype(BF16)
            le = le_ref[t] > 0.5
            s_all = dot_t(k_win, q_rows)
            s = jnp.where(le, s_all[:TOK], s_all[TOK:]) * (scale * math.log2(math.e)) + bias_ref[t, r]
            e = jnp.exp2(s - jnp.max(s, axis=0, keepdims=True))
            p = e * (1.0 / jnp.sum(e, axis=0, keepdims=True))
            d_all = dot_t(v_win, hg)
            d = jnp.where(le, d_all[:TOK], d_all[TOK:])
            ds = p * (d - jnp.sum(p * d, axis=0, keepdims=True))
            p2 = jnp.concatenate([jnp.where(le, p, 0.0), jnp.where(le, 0.0, p)], axis=0).astype(BF16)
            ds2 = jnp.concatenate([jnp.where(le, ds, 0.0), jnp.where(le, 0.0, ds)], axis=0).astype(BF16)
            attn = dot_tn(p2, v_win).astype(BF16).astype(F32)
            dq = dot_tn(ds2, k_win) * scale
            dv = dot_n(p2, hg)
            dk = dot_n(ds2, q_rows) * scale
            for g in range(GROUP):
                rows = slice(g * SIDE * WIDE, (g + 1) * SIDE * WIDE)
                cols = slice(g * DIM, (g + 1) * DIM)
                a_g = attn[rows].reshape(SIDE, WIDE, DIM)
                gacc[g] += jnp.sum(a_g * gin[u, :, r, :, cols].astype(F32), axis=0)
                att_o[u, :, r, :, cols] = (a_g * gains[h * GROUP + g : h * GROUP + g + 1, :]).astype(BF16)
                dq_o[u, :, r, :, cols] = dq[rows].reshape(SIDE, WIDE, DIM).astype(BF16)
            kp[u, :, :, before] = (kacc[...] + dk[TOK:]).reshape(SIDE, SIDE, WIDE, DIM).astype(BF16)
            vp[u, :, :, before] = (vacc[...] + dv[TOK:]).reshape(SIDE, SIDE, WIDE, DIM).astype(BF16)
            kacc[...] = dk[:TOK]
            vacc[...] = dv[:TOK]
            if u < 2:
                bulk(u, r, 1)
            return 0

        lax.fori_loop(0, OWN, one_round, 0)
        last = OWN - 1 + off(a)
        kp[u, :, :, last] = kacc[...].reshape(SIDE, SIDE, WIDE, DIM).astype(BF16)
        vp[u, :, :, last] = vacc[...].reshape(SIDE, SIDE, WIDE, DIM).astype(BF16)
        for k in (1, 3, 2):
            g, dev = g_peer(t, k)
            for n, (src, dst) in enumerate(((kp, kr), (vp, vr))):
                remote(src.at[u, g], dst.at[u, k - 1], rs_send.at[n], rs_recv.at[u, n], dev)
        for g in range(GROUP):
            gpart[u, g // 2, g % 2 : g % 2 + 1, :] = jnp.sum(gacc[g], axis=0, keepdims=True)
        gain_rows(u, True)

    def gain_rows(u, go):
        t, h = u % 2, UNIT_HEAD[u]
        if t == 0:

            @pl.when(z != h)
            def _():
                copy = pltpu.make_async_remote_copy(
                    src_ref=gpart.at[u], dst_ref=ghalf.at[u, (z - h + 3) % SIDE], send_sem=gr_send.at[u],
                    recv_sem=gr_recv.at[u], device_id=at_ctx(h * SIDE + x), device_id_type=MESH,
                )
                copy.start() if go else copy.wait_send()
        elif go:
            for k in (1, 3, 2):
                i, dev = g_peer(t, k)
                remote(gpart.at[u, i], ghalf.at[u, k - 1, 0], gr_send.at[u], gr_recv.at[u], dev)
        else:
            drain(gpart.at[u, pl.ds(0, SIDE - 1)], gr_send.at[u])

    def gain_cols(u, go):
        t, h = u % 2, UNIT_HEAD[u]
        if t == 0:

            @pl.when(z == h)
            def _():
                if go:
                    drain(ghalf.at[u], gr_recv.at[u])
                    gsum[u] = gpart[u] + ghalf[u, 0] + ghalf[u, 1] + ghalf[u, 2]
                    for k in (1, 3, 2):
                        i, dev = a_peer(t, k)
                        remote(gsum.at[u, i], gside.at[u, k - 1], ga_send.at[u], ga_recv.at[u], dev)
                else:
                    drain(gsum.at[u, pl.ds(0, SIDE - 1)], ga_send.at[u])
        else:
            if go:
                drain(ghalf.at[u, pl.ds(0, SIDE - 1), 0], gr_recv.at[u])
                gsum[u, x] = gpart[u, x] + ghalf[u, 0, 0] + ghalf[u, 1, 0] + ghalf[u, 2, 0]

            @pl.when(z != h)
            def _():
                copy = pltpu.make_async_remote_copy(
                    src_ref=gsum.at[u, x], dst_ref=gside.at[u, (z - h + 3) % SIDE], send_sem=ga_send.at[u],
                    recv_sem=ga_recv.at[u], device_id=at_ctx(h * SIDE + x), device_id_type=MESH,
                )
                copy.start() if go else copy.wait_send()

    def gain_over_dp(u):
        h = UNIT_HEAD[u]

        @pl.when(z == h)
        def _():
            drain(gside.at[u], ga_recv.at[u])
            gfin[...] = gsum[u, x] + gside[u, 0] + gside[u, 1] + gside[u, 2]
            for i in range(1, 8):
                remote(gfin, gdp.at[i - 1], d_send, d_recv, ((dp + i) % 8, ctx))

    def reduce_back(u):
        t = u % 2
        for n, (part, got, total, back) in enumerate(((kp, kr, ks, ka), (vp, vr, vs, va))):
            drain(got.at[u], rs_recv.at[u, n])
            acc = part[u, me_g(t)].astype(F32)
            for k in range(SIDE - 1):
                acc += got[u, k].astype(F32)
            total[u] = acc.astype(BF16)
            for k in (1, 3, 2):
                b, dev = a_peer(t, k)
                remote(total.at[u, b], back.at[u, me_a(t)], aa_send.at[n], aa_recv.at[u, n], dev)
            local(total.at[u, me_a(t)], back.at[u, me_a(t)], aa_recv.at[u, n])
        gain_cols(u, True)

    def finish(u):
        h = UNIT_HEAD[u]
        cols = slice(h * DIM, (h + 1) * DIM)
        for n, (back, out) in enumerate(((ka, dk_ref), (va, dv_ref))):
            drain(back.at[u], aa_recv.at[u, n])
            for rho in range(ROUNDS):
                b, r = rho // OWN, rho % OWN
                val = back[u, b, r if b == 0 else r + 1]
                if r == OWN - 1 and b < SIDE - 1:
                    val = (val.astype(F32) + back[u, b + 1, 0].astype(F32)).astype(BF16)
                out[0, rho, :, cols] = val

    unit(0)
    unit(1)
    reduce_back(0)
    unit(2)
    reduce_back(1)
    unit(3)
    bulk(2, 0, OWN)
    bulk(3, 0, OWN // 2)
    reduce_back(2)
    for u in range(2):
        gain_over_dp(u)
    reduce_back(3)
    bulk(3, OWN // 2, OWN // 2)
    gain_over_dp(2)
    for u in range(3):
        finish(u)
    gain_over_dp(3)
    finish(3)
    drain(gdp, d_recv)
    total = gfin[...]
    for i in range(7):
        total += gdp[i]
    gg_ref[...] = total * (1.0 / 128.0)
    for n, buf in enumerate((kin, vin)):
        drain(buf.at[:, 0, pl.ds(0, SIDE - 1)], kv_send.at[n])
        drain(buf.at[:, pl.ds(0, SIDE - 1)], kvg_send.at[n])
    for n, buf in enumerate((qin, gin)):
        drain(buf.at[:, pl.ds(0, SIDE - 1)], q_send.at[n])
    for n, buf in enumerate((kr, vr)):
        drain(buf, rs_send.at[n])
    for n, buf in enumerate((ka, va)):
        drain(buf.at[:, pl.ds(0, SIDE - 1)], aa_send.at[n])
    for n, (buf, dst) in enumerate(((att_o, att_hbm), (dq_o, dq_hbm))):
        drain(buf.at[:, pl.ds(0, SIDE - 1)], out_send.at[n])
        drain(dst, out_recv.at[n])
    for u in range(4):
        gain_rows(u, False)
        gain_cols(u, False)
    drain(gdp, d_send)


def write_out(att, dq, dk, dv, gg, att_out, dq_out, dk_out, dv_out, gg_out, big, small):
    copies = []
    for n, (src, dst) in enumerate(((att, att_out), (dq, dq_out))):
        for i in range(4):
            part = pl.ds(i * 4, 4)
            copies.append(pltpu.make_async_copy(src.at[:, part], dst.at[:, part], big.at[n, i]))
    for n, (src, dst) in enumerate(((dk, dk_out), (dv, dv_out))):
        copies.append(pltpu.make_async_copy(src, dst, small.at[n]))
    for copy in copies:
        copy.start()
    for i in range(2):
        gg_out[pl.ds(i * DIM, DIM)] = gg[i]
    for copy in copies:
        copy.wait()


def body(queries, key_rows, values, out_grad, out_gain, documents):
    queries, key_rows, values, out_grad, out_gain, documents = (
        pltpu.with_memory_space_constraint(a, pltpu.HBM)
        for a in (queries, key_rows, values, out_grad, out_gain, documents)
    )
    any_spec = pl.BlockSpec(memory_space=pl.ANY)
    vmem = pl.BlockSpec(memory_space=pltpu.VMEM)
    wide = pltpu.VMEM((4, SIDE, OWN, WIDE, GROUP * DIM), BF16)
    narrow = pltpu.VMEM((4, SIDE, SIDE, SLOTS, WIDE, DIM), BF16)
    narrow3 = pltpu.VMEM((4, SIDE - 1, SIDE, SLOTS, WIDE, DIM), BF16)
    flat = pltpu.VMEM((4, SIDE, SLOTS, WIDE, DIM), BF16)
    dma = pltpu.SemaphoreType.DMA
    att, dq, dk, dv, gg = pl.pallas_call(
        kernel,
        out_shape=(
            jax.ShapeDtypeStruct(queries.shape, BF16),
            jax.ShapeDtypeStruct(queries.shape, BF16),
            jax.ShapeDtypeStruct(key_rows.shape, BF16),
            jax.ShapeDtypeStruct(key_rows.shape, BF16),
            jax.ShapeDtypeStruct((2, DIM), F32),
        ),
        in_specs=[any_spec] * 6,
        out_specs=(any_spec, any_spec, vmem, vmem, vmem),
        scratch_shapes=[
            wide, wide, narrow, narrow, wide, wide, narrow, narrow, narrow3, narrow3, flat, flat, flat, flat,
            pltpu.VMEM(out_gain.shape, BF16),
            pltpu.VMEM(documents.shape, jnp.int32),
            pltpu.VMEM((2, TOK, ROWS), F32),
            pltpu.VMEM((2, OWN, TOK, ROWS), F32),
            pltpu.VMEM((TOK, DIM), F32),
            pltpu.VMEM((TOK, DIM), F32),
            pltpu.VMEM((GROUP, WIDE, DIM), F32),
            pltpu.VMEM((HEADS * GROUP, DIM), F32),
            pltpu.VMEM((4, SIDE, 2, DIM), F32),
            pltpu.VMEM((4, SIDE - 1, SIDE, 2, DIM), F32),
            pltpu.VMEM((4, SIDE, 2, DIM), F32),
            pltpu.VMEM((4, SIDE - 1, 2, DIM), F32),
            pltpu.VMEM((2, DIM), F32),
            pltpu.VMEM((7, 2, DIM), F32),
            dma((2,)), dma((4, 2)), dma((2,)), dma((4, 2)), dma((2,)), dma((4, 2)), dma((2,)), dma((2,)),
            dma((2,)), dma((4, 2)), dma((2,)), dma((4, 2)), dma((4,)), dma((4,)), dma((4,)), dma((4,)), dma, dma, dma((2,)),
        ],
        compiler_params=pltpu.CompilerParams(
            collective_id=0, has_side_effects=True, vmem_limit_bytes=48 * 1024 * 1024
        ),
        name="packed_attention",
    )(queries, key_rows, values, out_grad, out_gain, documents)
    return pl.pallas_call(
        write_out,
        out_shape=(
            jax.ShapeDtypeStruct(queries.shape, BF16),
            jax.ShapeDtypeStruct(queries.shape, BF16),
            jax.ShapeDtypeStruct(key_rows.shape, BF16),
            jax.ShapeDtypeStruct(key_rows.shape, BF16),
            jax.ShapeDtypeStruct((2 * DIM,), F32),
        ),
        in_specs=[any_spec] * 4 + [vmem],
        out_specs=(any_spec, any_spec, any_spec, any_spec, vmem),
        scratch_shapes=[dma((2, 4)), dma((2,))],
        compiler_params=pltpu.CompilerParams(vmem_limit_bytes=1024 * 1024),
        name="write_out",
    )(att, dq, dk, dv, gg)


def solution(mesh):
    tokens = P("dp", None, "ctx", None)
    return jax.shard_map(
        body,
        mesh=mesh,
        in_specs=(tokens, tokens, tokens, tokens, P(), P("dp", None)),
        out_specs=(tokens, tokens, tokens, tokens, P("ctx")),
        check_vma=False,
    )
```

```python
import functools
import math

import jax
import jax.numpy as jnp
from jax import lax
from jax.experimental import pallas as pl
from jax.experimental.pallas import tpu as pltpu
from jax.sharding import PartitionSpec as P

MESH = pl.DeviceIdType.MESH
F32 = jnp.float32
BF16 = jnp.bfloat16
SIDE = 4
ROUNDS = 16
OWN = ROUNDS // SIDE
SLOTS = OWN + 1
WIDE = 8
DIM = 128
GROUP = 8
HEADS = 4
TOK = 128
ROWS = SIDE * WIDE * GROUP
NEG_BIG = -1e30
UNIT_HEAD = (0, 2, 1, 3)


def dot_t(a, b):
    return lax.dot_general(a, b, (((1,), (1,)), ((), ())), preferred_element_type=F32)


def dot_tn(a, b):
    return lax.dot_general(a, b, (((0,), (0,)), ((), ())), preferred_element_type=F32)


def dot_n(a, b):
    return lax.dot_general(a, b, (((1,), (0,)), ((), ())), preferred_element_type=F32)


def kernel(
    q_hbm, k_hbm, v_hbm, g_hbm, gain_hbm, docs_hbm,
    att_hbm, dq_hbm, dk_ref, dv_ref, gg_ref,
    qin, gin, kin, vin, att_o, dq_o, kp, vp, kr, vr, ks, vs, ka, va,
    gain_ref, docs_ref, le_ref, bias_ref, kacc, vacc, gacc, gains, gpart, ghalf, gsum, gside, gfin, gdp,
    kv_send, kv_recv, kvg_send, kvg_recv, q_send, q_recv, out_send, out_recv,
    rs_send, rs_recv, aa_send, aa_recv, gr_send, gr_recv, ga_send, ga_recv, d_send, d_recv, small, hello,
):
    dp = lax.axis_index("dp")
    ctx = lax.axis_index("ctx")
    z = ctx // SIDE
    x = ctx % SIDE
    scale = 1.0 / math.sqrt(DIM)

    def at_ctx(c):
        return (dp, c)

    def a_peer(t, k):
        a = ((x if t == 0 else z) + k) % SIDE
        return a, at_ctx(z * SIDE + a if t == 0 else a * SIDE + x)

    def g_peer(t, k):
        g = ((z if t == 0 else x) + k) % SIDE
        return g, at_ctx(g * SIDE + x if t == 0 else z * SIDE + g)

    def me_a(t):
        return x if t == 0 else z

    def me_g(t):
        return z if t == 0 else x

    def off(a):
        return (a + SIDE - 1) // SIDE

    def remote(src, dst, ssem, rsem, dev):
        pltpu.make_async_remote_copy(
            src_ref=src, dst_ref=dst, send_sem=ssem, recv_sem=rsem, device_id=dev, device_id_type=MESH
        ).start()

    def local(src, dst, sem):
        pltpu.make_async_copy(src, dst, sem).start()

    def drain(ref, sem):
        pltpu.make_async_copy(ref, ref, sem).wait()

    barrier = pltpu.get_barrier_semaphore()
    for t in range(2):
        for k in range(1, SIDE):
            pl.semaphore_signal(barrier, inc=1, device_id=a_peer(t, k)[1], device_id_type=MESH)
    for i in range(1, 8):

        @pl.when(dp + i < 8)
        def _():
            pl.semaphore_signal(barrier, inc=1, device_id=(dp + i, ctx), device_id_type=MESH)


    def kv_local(u):
        t, h = u % 2, UNIT_HEAD[u]
        a = me_a(t)
        lanes = pl.ds(h * DIM, DIM)
        for n, (src, dst) in enumerate(((k_hbm, kin), (v_hbm, vin))):
            local(src.at[0, pl.ds(OWN * a - off(a), SLOTS), :, lanes], dst.at[u, me_g(t), a], kv_recv.at[u, n])

    def q_local(u):
        t, h = u % 2, UNIT_HEAD[u]
        a = me_a(t)
        lanes = pl.ds(h * GROUP * DIM, GROUP * DIM)
        for n, (src, dst) in enumerate(((q_hbm, qin), (g_hbm, gin))):
            local(src.at[0, pl.ds(OWN * a, OWN), :, lanes], dst.at[u, a], q_recv.at[u, n])

    def kv_first(pair):
        for k in (1, 3, 2):
            for n, (src, dst) in enumerate(((k_hbm, kin), (v_hbm, vin))):
                for u in pair:
                    t, h = u % 2, UNIT_HEAD[u]
                    a, dev = a_peer(t, k)
                    remote(
                        src.at[0, pl.ds(OWN * a - off(a), SLOTS), :, pl.ds(h * DIM, DIM)],
                        dst.at[u, me_g(t), me_a(t)], kv_send.at[n], kv_recv.at[u, n], dev,
                    )

    def kv_near(pair):
        for u in pair:
            for n, buf in enumerate((kin, vin)):
                drain(buf.at[u, 0], kv_recv.at[u, n])
        for k in (1, 3):
            for n, buf in enumerate((kin, vin)):
                for u in pair:
                    t = u % 2
                    _, dev = g_peer(t, k)
                    remote(buf.at[u, me_g(t)], buf.at[u, me_g(t)], kvg_send.at[n], kvg_recv.at[u, n, k - 1], dev)

    def kv_far(pair):
        for n, (buf, k) in enumerate(((kin, 1), (vin, 3))):
            for u in pair:
                t = u % 2
                drain(buf.at[u, 0], kvg_recv.at[u, n, k - 1])
                origin = (me_g(t) + SIDE - k) % SIDE
                _, dev = g_peer(t, k)
                remote(buf.at[u, origin], buf.at[u, origin], kvg_send.at[n], kvg_recv.at[u, n, 1], dev)

    def q_out(pair, n):
        src, dst = ((q_hbm, qin), (g_hbm, gin))[n]
        for k in (1, 3, 2):
            for u in pair:
                t, h = u % 2, UNIT_HEAD[u]
                a, dev = a_peer(t, k)
                remote(
                    src.at[0, pl.ds(OWN * a, OWN), :, pl.ds(h * GROUP * DIM, GROUP * DIM)],
                    dst.at[u, me_a(t)], q_send.at[n], q_recv.at[u, n], dev,
                )

    first, second = (0, 1), (2, 3)
    local(gain_hbm, gain_ref, small.at[0])
    local(docs_hbm, docs_ref, small.at[1])
    for u in range(4):
        kv_local(u)
    for u in range(4):
        q_local(u)
    pl.semaphore_wait(barrier, 6 + dp)
    for i in range(1, 8):

        @pl.when(dp >= i)
        def _():
            pl.semaphore_signal(hello, inc=1, device_id=(dp - i, ctx), device_id_type=MESH)

    kv_first(first)
    kv_first(second)
    q_out(first, 0)
    kv_near(first)
    kv_near(second)
    q_out(first, 1)
    kv_far(first)
    q_out(second, 0)
    kv_far(second)
    q_out(second, 1)

    drain(gain_ref, small.at[0])
    drain(docs_ref, small.at[1])
    for i in range(HEADS * GROUP):
        gains[i : i + 1, :] = gain_ref[pl.ds(i * DIM, DIM)].astype(F32).reshape(1, DIM)
    key_i = lax.broadcasted_iota(jnp.int32, (TOK, ROWS), 0)
    row_i = lax.broadcasted_iota(jnp.int32, (TOK, ROWS), 1) & (SIDE * WIDE - 1)
    for t in range(2):
        def key_col(i):
            return i if t == 0 else ((i >> 3) & 3) * 32 + (i >> 5) * 8 + (i & 7)

        def row_col(i):
            i = i & (SIDE * WIDE - 1)
            return z * 32 + i if t == 0 else (i >> 3) * 32 + x * 8 + (i & 7)

        le = key_col(key_i) <= row_col(row_i)
        le_ref[t] = jnp.where(le, 1.0, 0.0)
        perm = jnp.where(
            key_col(lax.broadcasted_iota(jnp.int32, (TOK, TOK), 0)) == lax.broadcasted_iota(jnp.int32, (TOK, TOK), 1),
            1.0, 0.0,
        ).astype(BF16)
        sel = jnp.where(
            row_col(lax.broadcasted_iota(jnp.int32, (ROWS, TOK), 0)) == lax.broadcasted_iota(jnp.int32, (ROWS, TOK), 1),
            1.0, 0.0,
        ).astype(BF16)

        def doc_row(r):
            return docs_ref[0:1, pl.ds(pl.multiple_of(r * TOK, TOK), TOK)].astype(F32)

        def one_bias(r, _):
            rho = me_a(t) * OWN + r
            cur = doc_row(rho)
            prev = doc_row((rho + ROUNDS - 1) % ROUNDS)
            k_cur = dot_t(perm, jnp.broadcast_to(cur, (ROWS, TOK)).astype(BF16))
            k_prev = dot_t(perm, jnp.broadcast_to(prev, (ROWS, TOK)).astype(BF16))
            q_doc = dot_t(jnp.broadcast_to(cur, (TOK, TOK)).astype(BF16), sel)
            k_prev = jnp.where(rho > 0, k_prev, -1.0)
            mine = jnp.where(le_ref[t] > 0.5, k_cur, k_prev)
            bias_ref[t, r] = jnp.where(mine == q_doc, 0.0, NEG_BIG)
            return 0

        lax.fori_loop(0, OWN, one_bias, 0)

    def bulk(pair, r, count):
        for n, (buf, dst) in enumerate(((att_o, att_hbm), (dq_o, dq_hbm))):
            for k in (1, 3, 2, 0):
                for u in pair:
                    t, h = u % 2, UNIT_HEAD[u]
                    there = dst.at[0, pl.ds(OWN * me_a(t) + r, count), :, pl.ds(h * GROUP * DIM, GROUP * DIM)]
                    b, dev = a_peer(t, k)
                    here = buf.at[u, b, pl.ds(r, count)]
                    if k:
                        remote(here, there, out_send.at[n], out_recv.at[n], dev)
                    else:
                        local(here, there, out_recv.at[n])

    def compute(pair, spread):
        for u in pair:
            for n, buf in enumerate((qin, gin)):
                drain(buf.at[u], q_recv.at[u, n])
            for n, (buf, rest) in enumerate(((kin, (2, 3)), (vin, (1, 2)))):
                for k in rest:
                    drain(buf.at[u, 0], kvg_recv.at[u, n, k - 1])
        kacc[...] = jnp.zeros_like(kacc)
        vacc[...] = jnp.zeros_like(vacc)
        gacc[...] = jnp.zeros_like(gacc)

        def one_round(u, r):
            t, h = u % 2, UNIT_HEAD[u]
            a = me_a(t)
            here = r + off(a)
            before = (here + SLOTS - 1) % SLOTS

            def keys(buf, s):
                return buf[u, :, :, s].astype(F32).reshape(TOK, DIM)

            k_win = jnp.concatenate([keys(kin, here), keys(kin, before)], axis=0).astype(BF16)
            v_win = jnp.concatenate([keys(vin, here), keys(vin, before)], axis=0).astype(BF16)
            q_rows = jnp.concatenate(
                [qin[u, :, r, :, g * DIM : (g + 1) * DIM].astype(F32).reshape(SIDE * WIDE, DIM) for g in range(GROUP)],
                axis=0,
            ).astype(BF16)
            hg = jnp.concatenate(
                [
                    gin[u, :, r, :, g * DIM : (g + 1) * DIM].astype(F32).reshape(SIDE * WIDE, DIM)
                    * gains[h * GROUP + g : h * GROUP + g + 1, :]
                    for g in range(GROUP)
                ],
                axis=0,
            ).astype(BF16)
            le = le_ref[t] > 0.5
            s_all = dot_t(k_win, q_rows)
            s = jnp.where(le, s_all[:TOK], s_all[TOK:]) * (scale * math.log2(math.e)) + bias_ref[t, r]
            e = jnp.exp2(s - jnp.max(s, axis=0, keepdims=True))
            p = e * (1.0 / jnp.sum(e, axis=0, keepdims=True))
            d_all = dot_t(v_win, hg)
            d = jnp.where(le, d_all[:TOK], d_all[TOK:])
            ds = p * (d - jnp.sum(p * d, axis=0, keepdims=True))
            p2 = jnp.concatenate([jnp.where(le, p, 0.0), jnp.where(le, 0.0, p)], axis=0).astype(BF16)
            ds2 = jnp.concatenate([jnp.where(le, ds, 0.0), jnp.where(le, 0.0, ds)], axis=0).astype(BF16)
            attn = dot_tn(p2, v_win).astype(BF16).astype(F32)
            dq = dot_tn(ds2, k_win) * scale
            dv = dot_n(p2, hg)
            dk = dot_n(ds2, q_rows) * scale
            for g in range(GROUP):
                rows = slice(g * SIDE * WIDE, (g + 1) * SIDE * WIDE)
                cols = slice(g * DIM, (g + 1) * DIM)
                a_g = attn[rows].reshape(SIDE, WIDE, DIM)
                gacc[t, g] += jnp.sum(a_g * gin[u, :, r, :, cols].astype(F32), axis=0)
                att_o[u, :, r, :, cols] = (a_g * gains[h * GROUP + g : h * GROUP + g + 1, :]).astype(BF16)
                dq_o[u, :, r, :, cols] = dq[rows].reshape(SIDE, WIDE, DIM).astype(BF16)
            kp[u, :, :, before] = (kacc[t] + dk[TOK:]).reshape(SIDE, SIDE, WIDE, DIM).astype(BF16)
            vp[u, :, :, before] = (vacc[t] + dv[TOK:]).reshape(SIDE, SIDE, WIDE, DIM).astype(BF16)
            kacc[t] = dk[:TOK]
            vacc[t] = dv[:TOK]

        def both(r, _):
            for u in pair:
                one_round(u, r)
            if spread:
                bulk(pair, r, 1)
            return 0

        lax.fori_loop(0, OWN, both, 0)
        for u in pair:
            t = u % 2
            last = OWN - 1 + off(me_a(t))
            kp[u, :, :, last] = kacc[t].reshape(SIDE, SIDE, WIDE, DIM).astype(BF16)
            vp[u, :, :, last] = vacc[t].reshape(SIDE, SIDE, WIDE, DIM).astype(BF16)
            for g in range(GROUP):
                gpart[u, g // 2, g % 2 : g % 2 + 1, :] = jnp.sum(gacc[t, g], axis=0, keepdims=True)

    def sums_near(pair):
        for n, (part, got, k) in enumerate(((kp, kr, 3), (vp, vr, 1))):
            for u in pair:
                t = u % 2
                _, dev = g_peer(t, SIDE - k)
                remote(part.at[u, (me_g(t) + 2) % SIDE], got.at[u, 1], rs_send.at[n], rs_recv.at[u, n, 1], dev)
        for n, (part, got, k) in enumerate(((kp, kr, 3), (vp, vr, 1))):
            for u in pair:
                g, dev = g_peer(u % 2, k)
                remote(part.at[u, g], got.at[u, 0], rs_send.at[n], rs_recv.at[u, n, 0], dev)
        for u in pair:
            gain_rows(u, True)

    def sums_far(pair):
        for n, (part, got, k) in enumerate(((kp, kr, 1), (vp, vr, 3))):
            for u in pair:
                g, dev = g_peer(u % 2, k)
                drain(got.at[u, 1], rs_recv.at[u, n, 1])
                got[u, 1] = (got[u, 1].astype(F32) + part[u, g].astype(F32)).astype(BF16)
                remote(got.at[u, 1], got.at[u, 2], rs_send.at[n], rs_recv.at[u, n, 2], dev)

    def gain_rows(u, go):
        t, h = u % 2, UNIT_HEAD[u]
        if t == 0:

            @pl.when(z != h)
            def _():
                copy = pltpu.make_async_remote_copy(
                    src_ref=gpart.at[u], dst_ref=ghalf.at[u, (z - h + 3) % SIDE], send_sem=gr_send.at[u],
                    recv_sem=gr_recv.at[u], device_id=at_ctx(h * SIDE + x), device_id_type=MESH,
                )
                copy.start() if go else copy.wait_send()
        elif go:
            for k in (1, 3, 2):
                i, dev = g_peer(t, k)
                remote(gpart.at[u, i], ghalf.at[u, k - 1, 0], gr_send.at[u], gr_recv.at[u], dev)
        else:
            drain(gpart.at[u, pl.ds(0, SIDE - 1)], gr_send.at[u])

    def gain_cols(u, go):
        t, h = u % 2, UNIT_HEAD[u]
        if t == 0:

            @pl.when(z == h)
            def _():
                if go:
                    drain(ghalf.at[u], gr_recv.at[u])
                    gsum[u] = gpart[u] + ghalf[u, 0] + ghalf[u, 1] + ghalf[u, 2]
                    for k in (1, 3, 2):
                        i, dev = a_peer(t, k)
                        remote(gsum.at[u, i], gside.at[u, k - 1], ga_send.at[u], ga_recv.at[u], dev)
                else:
                    drain(gsum.at[u, pl.ds(0, SIDE - 1)], ga_send.at[u])
        else:
            if go:
                drain(ghalf.at[u, pl.ds(0, SIDE - 1), 0], gr_recv.at[u])
                gsum[u, x] = gpart[u, x] + ghalf[u, 0, 0] + ghalf[u, 1, 0] + ghalf[u, 2, 0]

            @pl.when(z != h)
            def _():
                copy = pltpu.make_async_remote_copy(
                    src_ref=gsum.at[u, x], dst_ref=gside.at[u, (z - h + 3) % SIDE], send_sem=ga_send.at[u],
                    recv_sem=ga_recv.at[u], device_id=at_ctx(h * SIDE + x), device_id_type=MESH,
                )
                copy.start() if go else copy.wait_send()

    def gain_over_dp(u):
        h = UNIT_HEAD[u]

        @pl.when(z == h)
        def _():
            drain(gside.at[u], ga_recv.at[u])
            gfin[...] = gsum[u, x] + gside[u, 0] + gside[u, 1] + gside[u, 2]
            for i in range(1, 8):
                remote(gfin, gdp.at[i - 1], d_send, d_recv, ((dp + i) % 8, ctx))

    def sums_back(pair):
        for n, (part, got, total, back) in enumerate(((kp, kr, ks, ka), (vp, vr, vs, va))):
            for u in pair:
                drain(got.at[u, 0], rs_recv.at[u, n, 0])
                drain(got.at[u, 2], rs_recv.at[u, n, 2])
                total[u] = (
                    part[u, me_g(u % 2)].astype(F32) + got[u, 0].astype(F32) + got[u, 2].astype(F32)
                ).astype(BF16)
            for k in (1, 3, 2):
                for u in pair:
                    t = u % 2
                    b, dev = a_peer(t, k)
                    remote(total.at[u, b], back.at[u, me_a(t)], aa_send.at[n], aa_recv.at[u, n], dev)
            for u in pair:
                a = me_a(u % 2)
                local(total.at[u, a], back.at[u, a], aa_recv.at[u, n])

    def finish(u):
        h = UNIT_HEAD[u]
        cols = slice(h * DIM, (h + 1) * DIM)
        for n, (back, out) in enumerate(((ka, dk_ref), (va, dv_ref))):
            drain(back.at[u], aa_recv.at[u, n])
            for rho in range(ROUNDS):
                b, r = rho // OWN, rho % OWN
                val = back[u, b, r if b == 0 else r + 1]
                if r == OWN - 1 and b < SIDE - 1:
                    val = (val.astype(F32) + back[u, b + 1, 0].astype(F32)).astype(BF16)
                out[0, rho, :, cols] = val

    compute(first, False)
    sums_near(first)
    bulk(first, 0, 4)
    compute(second, False)
    sums_near(second)
    sums_far(first)
    for u in first:
        gain_cols(u, True)
    bulk(second, 0, 1)
    sums_far(second)
    for u in second:
        gain_cols(u, True)
    sums_back(first)

    @pl.when(dp < 7)
    def _():
        pl.semaphore_wait(hello, 7 - dp)

    for u in first:
        gain_over_dp(u)
    bulk(second, 1, 1)
    sums_back(second)
    for u in second:
        gain_over_dp(u)
    bulk(second, 2, 2)
    for u in range(4):
        finish(u)
    drain(gdp, d_recv)
    total = gfin[...]
    for i in range(7):
        total += gdp[i]
    gg_ref[...] = total * (1.0 / 128.0)
    for n, buf in enumerate((kin, vin)):
        drain(buf.at[:, 0, pl.ds(0, SIDE - 1)], kv_send.at[n])
        drain(buf.at[:, pl.ds(0, SIDE - 1)], kvg_send.at[n])
    for n, buf in enumerate((qin, gin)):
        drain(buf.at[:, pl.ds(0, SIDE - 1)], q_send.at[n])
    for n, buf in enumerate((kr, vr)):
        drain(buf, rs_send.at[n])
    for n, buf in enumerate((ka, va)):
        drain(buf.at[:, pl.ds(0, SIDE - 1)], aa_send.at[n])
    for n, (buf, dst) in enumerate(((att_o, att_hbm), (dq_o, dq_hbm))):
        drain(buf.at[:, pl.ds(0, SIDE - 1)], out_send.at[n])
        drain(dst, out_recv.at[n])
    for u in range(4):
        gain_rows(u, False)
        gain_cols(u, False)
    drain(gdp, d_send)


def write_out(att, dq, dk, dv, gg, att_out, dq_out, dk_out, dv_out, gg_out, big, small):
    copies = []
    for n, (src, dst) in enumerate(((att, att_out), (dq, dq_out))):
        for i in range(4):
            part = pl.ds(i * 4, 4)
            copies.append(pltpu.make_async_copy(src.at[:, part], dst.at[:, part], big.at[n, i]))
    for n, (src, dst) in enumerate(((dk, dk_out), (dv, dv_out))):
        copies.append(pltpu.make_async_copy(src, dst, small.at[n]))
    for copy in copies:
        copy.start()
    for i in range(2):
        gg_out[pl.ds(i * DIM, DIM)] = gg[i]
    for copy in copies:
        copy.wait()


def body(queries, key_rows, values, out_grad, out_gain, documents):
    queries, key_rows, values, out_grad, out_gain, documents = (
        pltpu.with_memory_space_constraint(a, pltpu.HBM)
        for a in (queries, key_rows, values, out_grad, out_gain, documents)
    )
    any_spec = pl.BlockSpec(memory_space=pl.ANY)
    vmem = pl.BlockSpec(memory_space=pltpu.VMEM)
    wide = pltpu.VMEM((4, SIDE, OWN, WIDE, GROUP * DIM), BF16)
    narrow = pltpu.VMEM((4, SIDE, SIDE, SLOTS, WIDE, DIM), BF16)
    narrow3 = pltpu.VMEM((4, SIDE - 1, SIDE, SLOTS, WIDE, DIM), BF16)
    flat = pltpu.VMEM((4, SIDE, SLOTS, WIDE, DIM), BF16)
    dma = pltpu.SemaphoreType.DMA
    att, dq, dk, dv, gg = pl.pallas_call(
        kernel,
        out_shape=(
            jax.ShapeDtypeStruct(queries.shape, BF16),
            jax.ShapeDtypeStruct(queries.shape, BF16),
            jax.ShapeDtypeStruct(key_rows.shape, BF16),
            jax.ShapeDtypeStruct(key_rows.shape, BF16),
            jax.ShapeDtypeStruct((2, DIM), F32),
        ),
        in_specs=[any_spec] * 6,
        out_specs=(any_spec, any_spec, vmem, vmem, vmem),
        scratch_shapes=[
            wide, wide, narrow, narrow, wide, wide, narrow, narrow, narrow3, narrow3, flat, flat, flat, flat,
            pltpu.VMEM(out_gain.shape, BF16),
            pltpu.VMEM(documents.shape, jnp.int32),
            pltpu.VMEM((2, TOK, ROWS), F32),
            pltpu.VMEM((2, OWN, TOK, ROWS), F32),
            pltpu.VMEM((2, TOK, DIM), F32),
            pltpu.VMEM((2, TOK, DIM), F32),
            pltpu.VMEM((2, GROUP, WIDE, DIM), F32),
            pltpu.VMEM((HEADS * GROUP, DIM), F32),
            pltpu.VMEM((4, SIDE, 2, DIM), F32),
            pltpu.VMEM((4, SIDE - 1, SIDE, 2, DIM), F32),
            pltpu.VMEM((4, SIDE, 2, DIM), F32),
            pltpu.VMEM((4, SIDE - 1, 2, DIM), F32),
            pltpu.VMEM((2, DIM), F32),
            pltpu.VMEM((7, 2, DIM), F32),
            dma((2,)), dma((4, 2)), dma((2,)), dma((4, 2, 3)), dma((2,)), dma((4, 2)), dma((2,)), dma((2,)),
            dma((2,)), dma((4, 2, 3)), dma((2,)), dma((4, 2)), dma((4,)), dma((4,)), dma((4,)), dma((4,)), dma, dma, dma((2,)), pltpu.SemaphoreType.REGULAR,
        ],
        compiler_params=pltpu.CompilerParams(
            collective_id=0, has_side_effects=True, vmem_limit_bytes=48 * 1024 * 1024
        ),
        name="packed_attention",
    )(queries, key_rows, values, out_grad, out_gain, documents)
    return pl.pallas_call(
        write_out,
        out_shape=(
            jax.ShapeDtypeStruct(queries.shape, BF16),
            jax.ShapeDtypeStruct(queries.shape, BF16),
            jax.ShapeDtypeStruct(key_rows.shape, BF16),
            jax.ShapeDtypeStruct(key_rows.shape, BF16),
            jax.ShapeDtypeStruct((2 * DIM,), F32),
        ),
        in_specs=[any_spec] * 4 + [vmem],
        out_specs=(any_spec, any_spec, any_spec, any_spec, vmem),
        scratch_shapes=[dma((2, 4)), dma((2,))],
        compiler_params=pltpu.CompilerParams(vmem_limit_bytes=1024 * 1024),
        name="write_out",
    )(att, dq, dk, dv, gg)


def solution(mesh):
    tokens = P("dp", None, "ctx", None)
    return jax.shard_map(
        body,
        mesh=mesh,
        in_specs=(tokens, tokens, tokens, tokens, P(), P("dp", None)),
        out_specs=(tokens, tokens, tokens, tokens, P("ctx")),
        check_vma=False,
    )
```

```python
import functools
import math

import jax
import jax.numpy as jnp
from jax import lax
from jax.experimental import pallas as pl
from jax.experimental.pallas import tpu as pltpu
from jax.sharding import PartitionSpec as P

MESH = pl.DeviceIdType.MESH
F32 = jnp.float32
BF16 = jnp.bfloat16
SIDE = 4
ROUNDS = 16
PART = ROUNDS // SIDE
SLOTS = 2 * PART + 1
WIDE = 8
DIM = 128
GROUP = 8
HEADS = 4
TOK = 128
ROWS = SIDE * WIDE * GROUP
NEG_BIG = -1e30
IN_SLOTS = ((0, 4), (0, 5), (4, 4), (5, 4))
OUT_SLOTS = ((0, 3), (0, 4), (3, 5), (4, 5))


def dot_t(a, b):
    return lax.dot_general(a, b, (((1,), (1,)), ((), ())), preferred_element_type=F32)


def dot_tn(a, b):
    return lax.dot_general(a, b, (((0,), (0,)), ((), ())), preferred_element_type=F32)


def dot_n(a, b):
    return lax.dot_general(a, b, (((1,), (0,)), ((), ())), preferred_element_type=F32)


def kernel(
    q_hbm, k_hbm, v_hbm, g_hbm, gain_hbm, docs_hbm,
    att_hbm, dq_hbm, dk_ref, dv_ref, gg_ref,
    qin, gin, kin, vin, att_o, dq_o, kp, vp, kr, vr, ks, vs, ka, va,
    kst, gain_ref, docs_ref, le_ref, bias_ref, kacc, vacc, gacc, gains, gpart, ghalf, gsum, gside, gdiag, gfin, gdp,
    kv_send, kv_recv, kvg_send, kvg_recv, q_send, q_recv, out_send, out_recv,
    rs_send, rs_recv, aa_send, aa_recv, gr_send, gr_recv, ga_send, ga_recv, d_send, d_recv, small, hello, kst_sem,
):
    dp = lax.axis_index("dp")
    ctx = lax.axis_index("ctx")
    z = ctx // SIDE
    x = ctx % SIDE
    scale = 1.0 / math.sqrt(DIM)

    def at_ctx(c):
        return (dp, c)

    def a_peer(t, k):
        a = ((x if t == 0 else z) + k) % SIDE
        return a, at_ctx(z * SIDE + a if t == 0 else a * SIDE + x)

    def g_peer(t, k):
        g = ((z if t == 0 else x) + k) % SIDE
        return g, at_ctx(g * SIDE + x if t == 0 else z * SIDE + g)

    def me_a(t):
        return x if t == 0 else z

    def me_g(t):
        return z if t == 0 else x

    def first_round(u):
        return 2 * PART * (u % 2) + PART * (u // 2)

    def lanes_of(h, width):
        return pl.ds(pl.multiple_of(h * width, width), width)

    def remote(src, dst, ssem, rsem, dev):
        pltpu.make_async_remote_copy(
            src_ref=src, dst_ref=dst, send_sem=ssem, recv_sem=rsem, device_id=dev, device_id_type=MESH
        ).start()

    def local(src, dst, sem):
        pltpu.make_async_copy(src, dst, sem).start()

    def drain(ref, sem):
        pltpu.make_async_copy(ref, ref, sem).wait()

    barrier = pltpu.get_barrier_semaphore()
    for t in range(2):
        for k in range(1, SIDE):
            pl.semaphore_signal(barrier, inc=1, device_id=a_peer(t, k)[1], device_id_type=MESH)
    for i in range(1, 8):

        @pl.when(dp + i < 8)
        def _():
            pl.semaphore_signal(barrier, inc=1, device_id=(dp + i, ctx), device_id_type=MESH)


    def key_rounds(u):
        start, count = IN_SLOTS[u]
        return pl.ds(start + (2 * PART - 1) * (u % 2), count), pl.ds(start, count)

    def kv_local(u):
        t = u % 2
        a = me_a(t)
        rounds, slots = key_rounds(u)
        for n, (src, dst) in enumerate(((k_hbm, kin), (v_hbm, vin))):
            local(src.at[0, rounds, :, lanes_of(a, DIM)], dst.at[t, me_g(t), a, slots], kv_recv.at[u, n])

    def q_local(u):
        a = me_a(u % 2)
        for n, (src, dst) in enumerate(((q_hbm, qin), (g_hbm, gin))):
            local(
                src.at[0, pl.ds(first_round(u), PART), :, lanes_of(a, GROUP * DIM)], dst.at[u, a], q_recv.at[u, n]
            )

    def kv_first(pair):
        for k in (1, 3, 2):
            for n, dst in enumerate((kin, vin)):
                for u in pair:
                    t = u % 2
                    rounds, slots = key_rounds(u)
                    a, dev = a_peer(t, k)
                    remote(
                        kst.at[n, a, rounds], dst.at[t, me_g(t), me_a(t), slots], kv_send.at[u, n], kv_recv.at[u, n], dev
                    )

    def kv_near(pair):
        for u in pair:
            slots = key_rounds(u)[1]
            for n, buf in enumerate((kin, vin)):
                drain(buf.at[u % 2, 0, :, slots], kv_recv.at[u, n])
        for k in (1, 3):
            for n, buf in enumerate((kin, vin)):
                for u in pair:
                    t = u % 2
                    block = buf.at[t, me_g(t), :, key_rounds(u)[1]]
                    remote(block, block, kvg_send.at[u, n], kvg_recv.at[u, n, k - 1], g_peer(t, k)[1])

    def kv_far(pair):
        for n, (buf, k) in enumerate(((kin, 1), (vin, 3))):
            for u in pair:
                t = u % 2
                slots = key_rounds(u)[1]
                drain(buf.at[t, 0, :, slots], kvg_recv.at[u, n, k - 1])
                block = buf.at[t, (me_g(t) + SIDE - k) % SIDE, :, slots]
                remote(block, block, kvg_send.at[u, n], kvg_recv.at[u, n, 1], g_peer(t, k)[1])

    def q_out(pair, n):
        src, dst = ((q_hbm, qin), (g_hbm, gin))[n]
        for k in (1, 3, 2):
            for u in pair:
                t = u % 2
                a, dev = a_peer(t, k)
                remote(
                    src.at[0, pl.ds(first_round(u), PART), :, lanes_of(a, GROUP * DIM)],
                    dst.at[u, me_a(t)], q_send.at[n], q_recv.at[u, n], dev,
                )

    first, second = (0, 1), (2, 3)
    for h in range(HEADS):
        for n, src in enumerate((k_hbm, v_hbm)):
            local(src.at[0, :, :, pl.ds(h * DIM, DIM)], kst.at[n, h], kst_sem)
    pl.semaphore_wait(barrier, 6 + dp)
    drain(kst, kst_sem)
    kv_first(first)
    kv_first(second)
    q_out(first, 0)
    for i in range(1, 8):

        @pl.when(dp >= i)
        def _():
            pl.semaphore_signal(hello, inc=1, device_id=(dp - i, ctx), device_id_type=MESH)

    local(gain_hbm, gain_ref, small.at[0])
    local(docs_hbm, docs_ref, small.at[1])
    for u in range(4):
        kv_local(u)
    for u in range(4):
        q_local(u)
    kv_near(first)
    kv_near(second)
    q_out(first, 1)
    kv_far(first)
    q_out(second, 0)
    kv_far(second)
    q_out(second, 1)

    drain(gain_ref, small.at[0])
    drain(docs_ref, small.at[1])
    for i in range(HEADS * GROUP):
        gains[i : i + 1, :] = gain_ref[pl.ds(i * DIM, DIM)].astype(F32).reshape(1, DIM)
    key_i = lax.broadcasted_iota(jnp.int32, (TOK, ROWS), 0)
    row_i = lax.broadcasted_iota(jnp.int32, (TOK, ROWS), 1) & (SIDE * WIDE - 1)
    for t in range(2):
        def key_col(i):
            return i if t == 0 else ((i >> 3) & 3) * 32 + (i >> 5) * 8 + (i & 7)

        def row_col(i):
            i = i & (SIDE * WIDE - 1)
            return z * 32 + i if t == 0 else (i >> 3) * 32 + x * 8 + (i & 7)

        le = key_col(key_i) <= row_col(row_i)
        le_ref[t] = jnp.where(le, 1.0, 0.0)
        perm = jnp.where(
            key_col(lax.broadcasted_iota(jnp.int32, (TOK, TOK), 0)) == lax.broadcasted_iota(jnp.int32, (TOK, TOK), 1),
            1.0, 0.0,
        ).astype(BF16)
        sel = jnp.where(
            row_col(lax.broadcasted_iota(jnp.int32, (ROWS, TOK), 0)) == lax.broadcasted_iota(jnp.int32, (ROWS, TOK), 1),
            1.0, 0.0,
        ).astype(BF16)

        def doc_row(r):
            return docs_ref[0:1, pl.ds(pl.multiple_of(r * TOK, TOK), TOK)].astype(F32)

        def one_bias(r, _):
            rho = 2 * PART * t + r
            cur = doc_row(rho)
            prev = doc_row((rho + ROUNDS - 1) % ROUNDS)
            k_cur = dot_t(perm, jnp.broadcast_to(cur, (ROWS, TOK)).astype(BF16))
            k_prev = dot_t(perm, jnp.broadcast_to(prev, (ROWS, TOK)).astype(BF16))
            q_doc = dot_t(jnp.broadcast_to(cur, (TOK, TOK)).astype(BF16), sel)
            k_prev = jnp.where(rho > 0, k_prev, -1.0)
            mine = jnp.where(le_ref[t] > 0.5, k_cur, k_prev)
            bias_ref[t, r] = jnp.where(mine == q_doc, 0.0, NEG_BIG)
            return 0

        lax.fori_loop(0, 2 * PART, one_bias, 0)

    def bulk(pair, r, count):
        for n, (buf, dst) in enumerate(((att_o, att_hbm), (dq_o, dq_hbm))):
            for k in (1, 3, 2, 0):
                for u in pair:
                    t = u % 2
                    there = dst.at[0, pl.ds(first_round(u) + r, count), :, lanes_of(me_a(t), GROUP * DIM)]
                    b, dev = a_peer(t, k)
                    here = buf.at[u, b, pl.ds(r, count)]
                    if k:
                        remote(here, there, out_send.at[n], out_recv.at[n], dev)
                    else:
                        local(here, there, out_recv.at[n])

    def compute(pair):
        for u in pair:
            slots = key_rounds(u)[1]
            for n, buf in enumerate((qin, gin)):
                drain(buf.at[u], q_recv.at[u, n])
            for n, (buf, rest) in enumerate(((kin, (2, 3)), (vin, (1, 2)))):
                for k in rest:
                    drain(buf.at[u % 2, 0, :, slots], kvg_recv.at[u, n, k - 1])

        def one_round(u, r):
            t = u % 2
            h = me_a(t)
            here = PART * (u // 2) + r + t
            before = here - ((r + PART - 1) // PART if u == 0 else 1)

            def gain_row(g):
                return gains[pl.ds(h * GROUP + g, 1), :]

            def keys(buf, s):
                return buf[t, :, :, s].astype(F32).reshape(TOK, DIM)

            k_win = jnp.concatenate([keys(kin, here), keys(kin, before)], axis=0).astype(BF16)
            v_win = jnp.concatenate([keys(vin, here), keys(vin, before)], axis=0).astype(BF16)
            q_rows = jnp.concatenate(
                [qin[u, :, r, :, g * DIM : (g + 1) * DIM].astype(F32).reshape(SIDE * WIDE, DIM) for g in range(GROUP)],
                axis=0,
            ).astype(BF16)
            hg = jnp.concatenate(
                [
                    gin[u, :, r, :, g * DIM : (g + 1) * DIM].astype(F32).reshape(SIDE * WIDE, DIM)
                    * gain_row(g)
                    for g in range(GROUP)
                ],
                axis=0,
            ).astype(BF16)
            le = le_ref[t] > 0.5
            s_all = dot_t(k_win, q_rows)
            s = jnp.where(le, s_all[:TOK], s_all[TOK:]) * (scale * math.log2(math.e)) + bias_ref[t, PART * (u // 2) + r]
            e = jnp.exp2(s - jnp.max(s, axis=0, keepdims=True))
            p = e * (1.0 / jnp.sum(e, axis=0, keepdims=True))
            d_all = dot_t(v_win, hg)
            d = jnp.where(le, d_all[:TOK], d_all[TOK:])
            ds = p * (d - jnp.sum(p * d, axis=0, keepdims=True))
            p2 = jnp.concatenate([jnp.where(le, p, 0.0), jnp.where(le, 0.0, p)], axis=0).astype(BF16)
            ds2 = jnp.concatenate([jnp.where(le, ds, 0.0), jnp.where(le, 0.0, ds)], axis=0).astype(BF16)
            attn = dot_tn(p2, v_win).astype(BF16).astype(F32)
            dq = dot_tn(ds2, k_win) * scale
            dv = dot_n(p2, hg)
            dk = dot_n(ds2, q_rows) * scale
            for g in range(GROUP):
                rows = slice(g * SIDE * WIDE, (g + 1) * SIDE * WIDE)
                cols = slice(g * DIM, (g + 1) * DIM)
                a_g = attn[rows].reshape(SIDE, WIDE, DIM)
                gacc[t, g] += jnp.sum(a_g * gin[u, :, r, :, cols].astype(F32), axis=0)
                att_o[u, :, r, :, cols] = (a_g * gain_row(g)).astype(BF16)
                dq_o[u, :, r, :, cols] = dq[rows].reshape(SIDE, WIDE, DIM).astype(BF16)
            kp[t, :, :, before] = (kacc[t] + dk[TOK:]).reshape(SIDE, SIDE, WIDE, DIM).astype(BF16)
            vp[t, :, :, before] = (vacc[t] + dv[TOK:]).reshape(SIDE, SIDE, WIDE, DIM).astype(BF16)
            kacc[t] = dk[:TOK]
            vacc[t] = dv[:TOK]

        def both(r, _):
            for u in pair:
                one_round(u, r)
            return 0

        lax.fori_loop(0, PART, both, 0)

    def end_of_rounds():
        for t in range(2):
            last = 2 * PART - 1 + t
            kp[t, :, :, last] = kacc[t].reshape(SIDE, SIDE, WIDE, DIM).astype(BF16)
            vp[t, :, :, last] = vacc[t].reshape(SIDE, SIDE, WIDE, DIM).astype(BF16)
            for g in range(GROUP):
                gpart[t, g // 2, g % 2 : g % 2 + 1, :] = jnp.sum(gacc[t, g], axis=0, keepdims=True)

    def grad_slots(u):
        return pl.ds(*OUT_SLOTS[u])

    def sums_near(pair):
        for n, (part, got, k) in enumerate(((kp, kr, 3), (vp, vr, 1))):
            for u in pair:
                t, slots = u % 2, grad_slots(u)
                remote(
                    part.at[t, (me_g(t) + 2) % SIDE, :, slots], got.at[t, 1, :, slots],
                    rs_send.at[u, n], rs_recv.at[u, n, 1], g_peer(t, SIDE - k)[1],
                )
        for n, (part, got, k) in enumerate(((kp, kr, 3), (vp, vr, 1))):
            for u in pair:
                t, slots = u % 2, grad_slots(u)
                g, dev = g_peer(t, k)
                remote(
                    part.at[t, g, :, slots], got.at[t, 0, :, slots], rs_send.at[u, n], rs_recv.at[u, n, 0], dev
                )

    def sums_far(pair):
        for n, (part, got, k) in enumerate(((kp, kr, 1), (vp, vr, 3))):
            for u in pair:
                t, slots = u % 2, grad_slots(u)
                g, dev = g_peer(t, k)
                drain(got.at[t, 1, :, slots], rs_recv.at[u, n, 1])
                got[t, 1, :, slots] = (
                    got[t, 1, :, slots].astype(F32) + part[t, g, :, slots].astype(F32)
                ).astype(BF16)
                remote(
                    got.at[t, 1, :, slots], got.at[t, 2, :, slots], rs_send.at[u, n], rs_recv.at[u, n, 2], dev
                )

    def sums_back(pair):
        for n, (part, got, total, back) in enumerate(((kp, kr, ks, ka), (vp, vr, vs, va))):
            for u in pair:
                t, slots = u % 2, grad_slots(u)
                drain(got.at[t, 0, :, slots], rs_recv.at[u, n, 0])
                drain(got.at[t, 2, :, slots], rs_recv.at[u, n, 2])
                total[t, :, slots] = (
                    part[t, me_g(t), :, slots].astype(F32)
                    + got[t, 0, :, slots].astype(F32)
                    + got[t, 2, :, slots].astype(F32)
                ).astype(BF16)
            for k in (1, 3, 2):
                for u in pair:
                    t, slots = u % 2, grad_slots(u)
                    b, dev = a_peer(t, k)
                    remote(
                        total.at[t, b, slots], back.at[t, me_a(t), slots], aa_send.at[u, n], aa_recv.at[u, n], dev
                    )
            for u in pair:
                t, slots = u % 2, grad_slots(u)
                local(total.at[t, me_a(t), slots], back.at[t, me_a(t), slots], aa_recv.at[u, n])

    def gain_rows(go):
        @pl.when(z != x)
        def _():
            copy = pltpu.make_async_remote_copy(
                src_ref=gpart.at[0], dst_ref=ghalf.at[(z - x + 3) % SIDE], send_sem=gr_send.at[0],
                recv_sem=gr_recv.at[0], device_id=at_ctx(x * SIDE + x), device_id_type=MESH,
            )
            copy.start() if go else copy.wait_send()

        if go:
            for k in (1, 3, 2):
                i, dev = g_peer(1, k)
                remote(gpart.at[1, i], gside.at[k - 1], gr_send.at[1], gr_recv.at[1], dev)
        else:
            drain(gpart.at[1, pl.ds(0, SIDE - 1)], gr_send.at[1])

    def gain_cols(go):
        @pl.when(z == x)
        def _():
            if go:
                drain(ghalf, gr_recv.at[0])
                gsum[...] = gpart[0] + ghalf[0] + ghalf[1] + ghalf[2]
                for k in (1, 3, 2):
                    i, dev = g_peer(1, k)
                    remote(gsum.at[i], gdiag, ga_send, ga_recv, dev)
                gdiag[...] = gsum[x]
            else:
                drain(gsum.at[pl.ds(0, SIDE - 1)], ga_send)

    def gain_over_dp():
        drain(gside, gr_recv.at[1])

        @pl.when(z != x)
        def _():
            drain(gdiag, ga_recv)

        gfin[...] = gdiag[...] + gpart[1, x] + gside[0] + gside[1] + gside[2]
        for i in range(1, 8):
            remote(gfin, gdp.at[i - 1], d_send, d_recv, ((dp + i) % 8, ctx))

    def finish(pair):
        for n, (back, out) in enumerate(((ka, dk_ref), (va, dv_ref))):
            for u in pair:
                t = u % 2
                drain(back.at[t, :, grad_slots(u)], aa_recv.at[u, n])
            for u in pair:
                t = u % 2
                start, count = OUT_SLOTS[u]
                for slot in range(start, start + count):
                    rho = slot + (2 * PART - 1) * t
                    if t == 1 and slot == 0:
                        continue
                    for h in range(HEADS):
                        val = back[t, h, slot]
                        if t == 0 and slot == 2 * PART - 1:
                            val = (val.astype(F32) + back[1, h, 0].astype(F32)).astype(BF16)
                        out[0, rho, :, h * DIM : (h + 1) * DIM] = val

    kacc[...] = jnp.zeros_like(kacc)
    vacc[...] = jnp.zeros_like(vacc)
    gacc[...] = jnp.zeros_like(gacc)
    compute(first)
    sums_near(first)
    bulk(first, 0, PART)
    compute(second)
    end_of_rounds()
    sums_near(second)
    gain_rows(True)
    sums_far(first)
    bulk(second, 0, 1)
    sums_far(second)
    gain_cols(True)
    sums_back(first)
    bulk(second, 1, 1)

    @pl.when(dp < 7)
    def _():
        pl.semaphore_wait(hello, 7 - dp)

    gain_over_dp()
    sums_back(second)
    bulk(second, 2, 2)
    finish(first)
    finish(second)
    drain(gdp, d_recv)
    total = gfin[...]
    for i in range(7):
        total += gdp[i]
    for i in range(2):
        gg_ref[pl.ds(i * DIM, DIM)] = total[i] * (1.0 / 128.0)
    for u in range(4):
        t, slots, grads = u % 2, key_rounds(u)[1], grad_slots(u)
        for n, buf in enumerate((kin, vin)):
            drain(buf.at[t, 0, pl.ds(0, SIDE - 1), slots], kv_send.at[u, n])
            drain(buf.at[t, pl.ds(0, SIDE - 1), :, slots], kvg_send.at[u, n])
        for n, (got, back) in enumerate(((kr, ka), (vr, va))):
            drain(got.at[t, :, :, grads], rs_send.at[u, n])
            drain(back.at[t, pl.ds(0, SIDE - 1), grads], aa_send.at[u, n])
    for n, buf in enumerate((qin, gin)):
        drain(buf.at[:, pl.ds(0, SIDE - 1)], q_send.at[n])
    for n, (buf, dst) in enumerate(((att_o, att_hbm), (dq_o, dq_hbm))):
        drain(buf.at[:, pl.ds(0, SIDE - 1)], out_send.at[n])
        drain(dst, out_recv.at[n])
    gain_rows(False)
    gain_cols(False)
    drain(gdp, d_send)


def write_out(att, dq, dk, dv, gg, att_out, dq_out, dk_out, dv_out, gg_out, big, small):
    copies = []
    for n, (src, dst) in enumerate(((att, att_out), (dq, dq_out))):
        for i in range(4):
            part = pl.ds(i * 4, 4)
            copies.append(pltpu.make_async_copy(src.at[:, part], dst.at[:, part], big.at[n, i]))
    for n, (src, dst) in enumerate(((dk, dk_out), (dv, dv_out), (gg, gg_out))):
        copies.append(pltpu.make_async_copy(src, dst, small.at[n]))
    for copy in copies:
        copy.start()
    for copy in copies:
        copy.wait()


def body(queries, key_rows, values, out_grad, out_gain, documents):
    queries, key_rows, values, out_grad, out_gain, documents = (
        pltpu.with_memory_space_constraint(a, pltpu.HBM)
        for a in (queries, key_rows, values, out_grad, out_gain, documents)
    )
    any_spec = pl.BlockSpec(memory_space=pl.ANY)
    vmem = pl.BlockSpec(memory_space=pltpu.VMEM)
    wide = pltpu.VMEM((4, SIDE, PART, WIDE, GROUP * DIM), BF16)
    narrow = pltpu.VMEM((2, SIDE, SIDE, SLOTS, WIDE, DIM), BF16)
    narrow3 = pltpu.VMEM((2, SIDE - 1, SIDE, SLOTS, WIDE, DIM), BF16)
    flat = pltpu.VMEM((2, SIDE, SLOTS, WIDE, DIM), BF16)
    dma = pltpu.SemaphoreType.DMA
    att, dq, dk, dv, gg = pl.pallas_call(
        kernel,
        out_shape=(
            jax.ShapeDtypeStruct(queries.shape, BF16),
            jax.ShapeDtypeStruct(queries.shape, BF16),
            jax.ShapeDtypeStruct(key_rows.shape, BF16),
            jax.ShapeDtypeStruct(key_rows.shape, BF16),
            jax.ShapeDtypeStruct((2 * DIM,), F32),
        ),
        in_specs=[any_spec] * 6,
        out_specs=(any_spec, any_spec, vmem, vmem, vmem),
        scratch_shapes=[
            wide, wide, narrow, narrow, wide, wide, narrow, narrow, narrow3, narrow3, flat, flat, flat, flat,
            pltpu.VMEM((2, 4, ROUNDS, WIDE, DIM), BF16),
            pltpu.VMEM(out_gain.shape, BF16),
            pltpu.VMEM(documents.shape, jnp.int32),
            pltpu.VMEM((2, TOK, ROWS), F32),
            pltpu.VMEM((2, 2 * PART, TOK, ROWS), F32),
            pltpu.VMEM((2, TOK, DIM), F32),
            pltpu.VMEM((2, TOK, DIM), F32),
            pltpu.VMEM((2, GROUP, WIDE, DIM), F32),
            pltpu.VMEM((HEADS * GROUP, DIM), F32),
            pltpu.VMEM((2, SIDE, 2, DIM), F32),
            pltpu.VMEM((SIDE - 1, SIDE, 2, DIM), F32),
            pltpu.VMEM((SIDE, 2, DIM), F32),
            pltpu.VMEM((SIDE - 1, 2, DIM), F32),
            pltpu.VMEM((2, DIM), F32),
            pltpu.VMEM((2, DIM), F32),
            pltpu.VMEM((7, 2, DIM), F32),
            dma((4, 2)), dma((4, 2)), dma((4, 2)), dma((4, 2, 3)), dma((2,)), dma((4, 2)), dma((2,)), dma((2,)),
            dma((4, 2)), dma((4, 2, 3)), dma((4, 2)), dma((4, 2)), dma((2,)), dma((2,)), dma, dma, dma, dma,
            dma((2,)), pltpu.SemaphoreType.REGULAR, dma,
        ],
        compiler_params=pltpu.CompilerParams(
            collective_id=0, has_side_effects=True, vmem_limit_bytes=48 * 1024 * 1024
        ),
        name="packed_attention",
    )(queries, key_rows, values, out_grad, out_gain, documents)
    return pl.pallas_call(
        write_out,
        out_shape=(
            jax.ShapeDtypeStruct(queries.shape, BF16),
            jax.ShapeDtypeStruct(queries.shape, BF16),
            jax.ShapeDtypeStruct(key_rows.shape, BF16),
            jax.ShapeDtypeStruct(key_rows.shape, BF16),
            jax.ShapeDtypeStruct((2 * DIM,), F32),
        ),
        in_specs=[any_spec] * 5,
        out_specs=(any_spec,) * 5,
        scratch_shapes=[dma((2, 4)), dma((3,))],
        compiler_params=pltpu.CompilerParams(vmem_limit_bytes=1024 * 1024),
        name="write_out",
    )(att, dq, dk, dv, gg)


def solution(mesh):
    tokens = P("dp", None, "ctx", None)
    return jax.shard_map(
        body,
        mesh=mesh,
        in_specs=(tokens, tokens, tokens, tokens, P(), P("dp", None)),
        out_specs=(tokens, tokens, tokens, tokens, P("ctx")),
        check_vma=False,
    )
```

```python
import functools
import math

import jax
import jax.numpy as jnp
from jax import lax
from jax.experimental import pallas as pl
from jax.experimental.pallas import tpu as pltpu
from jax.sharding import PartitionSpec as P

MESH = pl.DeviceIdType.MESH
F32 = jnp.float32
BF16 = jnp.bfloat16
SIDE = 4
ROUNDS = 16
PART = ROUNDS // SIDE
SLOTS = 2 * PART + 1
WIDE = 8
DIM = 128
GROUP = 8
HEADS = 4
TOK = 128
ROWS = SIDE * WIDE * GROUP
NEG_BIG = -1e30
IN_SLOTS = ((0, 4), (0, 5), (4, 4), (5, 4))
OUT_SLOTS = ((0, 3), (0, 4), (3, 5), (4, 5))


def dot_t(a, b):
    return lax.dot_general(a, b, (((1,), (1,)), ((), ())), preferred_element_type=F32)


def dot_tn(a, b):
    return lax.dot_general(a, b, (((0,), (0,)), ((), ())), preferred_element_type=F32)


def dot_n(a, b):
    return lax.dot_general(a, b, (((1,), (0,)), ((), ())), preferred_element_type=F32)


def kernel(
    q_hbm, k_hbm, v_hbm, g_hbm, gain_hbm, docs_hbm,
    att_hbm, dq_hbm, dk_ref, dv_ref, gg_ref,
    qin, gin, kin, vin, att_o, dq_o, kp, vp, kr, vr, ks, vs, ka, va,
    kst, gain_ref, docs_ref, le_ref, bias_ref, kacc, vacc, gacc, gains, gpart, ghalf, gsum, gside, gdiag, gfin, gdp,
    kv_send, kv_recv, kvg_send, kvg_recv, q_send, q_recv, out_send, out_recv,
    rs_send, rs_recv, aa_send, aa_recv, gr_send, gr_recv, ga_send, ga_recv, d_send, d_recv, small, hello, kst_sem,
):
    dp = lax.axis_index("dp")
    ctx = lax.axis_index("ctx")
    z = ctx // SIDE
    x = ctx % SIDE
    scale = 1.0 / math.sqrt(DIM)

    def at_ctx(c):
        return (dp, c)

    core = dp % 2

    def over_x(t):
        return 1 - core if t == 0 else core

    def me_a(t):
        return over_x(t) * x + (1 - over_x(t)) * z

    def me_g(t):
        return over_x(t) * z + (1 - over_x(t)) * x

    def device(t, a, g):
        return at_ctx(over_x(t) * (g * SIDE + a) + (1 - over_x(t)) * (a * SIDE + g))

    def a_peer(t, k):
        a = (me_a(t) + k) % SIDE
        return a, device(t, a, me_g(t))

    def g_peer(t, k):
        g = (me_g(t) + k) % SIDE
        return g, device(t, me_a(t), g)

    def x_peer(k):
        i = (x + k) % SIDE
        return i, at_ctx(z * SIDE + i)

    def first_round(u):
        return 2 * PART * (u % 2) + PART * (u // 2)

    def lanes_of(h, width):
        return pl.ds(pl.multiple_of(h * width, width), width)

    def remote(src, dst, ssem, rsem, dev):
        pltpu.make_async_remote_copy(
            src_ref=src, dst_ref=dst, send_sem=ssem, recv_sem=rsem, device_id=dev, device_id_type=MESH
        ).start()

    def local(src, dst, sem):
        pltpu.make_async_copy(src, dst, sem).start()

    def drain(ref, sem):
        pltpu.make_async_copy(ref, ref, sem).wait()

    barrier = pltpu.get_barrier_semaphore()
    for t in range(2):
        for k in range(1, SIDE):
            pl.semaphore_signal(barrier, inc=1, device_id=a_peer(t, k)[1], device_id_type=MESH)
    for i in range(1, 8):

        @pl.when(dp + i < 8)
        def _():
            pl.semaphore_signal(barrier, inc=1, device_id=(dp + i, ctx), device_id_type=MESH)


    def key_rounds(u):
        start, count = IN_SLOTS[u]
        return pl.ds(start + (2 * PART - 1) * (u % 2), count), pl.ds(start, count)

    def kv_local(u):
        t = u % 2
        a = me_a(t)
        rounds, slots = key_rounds(u)
        for n, (src, dst) in enumerate(((k_hbm, kin), (v_hbm, vin))):
            local(src.at[0, rounds, :, lanes_of(a, DIM)], dst.at[t, me_g(t), a, slots], kv_recv.at[u, n])

    def q_local(u):
        a = me_a(u % 2)
        for n, (src, dst) in enumerate(((q_hbm, qin), (g_hbm, gin))):
            local(
                src.at[0, pl.ds(first_round(u), PART), :, lanes_of(a, GROUP * DIM)], dst.at[u, a], q_recv.at[u, n]
            )

    def kv_first(pair):
        for k in (1, 3, 2):
            for n, dst in enumerate((kin, vin)):
                for u in pair:
                    t = u % 2
                    rounds, slots = key_rounds(u)
                    a, dev = a_peer(t, k)
                    remote(
                        kst.at[n, a, rounds], dst.at[t, me_g(t), me_a(t), slots], kv_send.at[u, n], kv_recv.at[u, n], dev
                    )

    def kv_near(pair):
        for u in pair:
            slots = key_rounds(u)[1]
            for n, buf in enumerate((kin, vin)):
                drain(buf.at[u % 2, 0, :, slots], kv_recv.at[u, n])
        for k in (1, 3):
            for n, buf in enumerate((kin, vin)):
                for u in pair:
                    t = u % 2
                    block = buf.at[t, me_g(t), :, key_rounds(u)[1]]
                    remote(block, block, kvg_send.at[u, n], kvg_recv.at[u, n, k - 1], g_peer(t, k)[1])

    def kv_far(pair):
        for n, (buf, k) in enumerate(((kin, 1), (vin, 3))):
            for u in pair:
                t = u % 2
                slots = key_rounds(u)[1]
                drain(buf.at[t, 0, :, slots], kvg_recv.at[u, n, k - 1])
                block = buf.at[t, (me_g(t) + SIDE - k) % SIDE, :, slots]
                remote(block, block, kvg_send.at[u, n], kvg_recv.at[u, n, 1], g_peer(t, k)[1])

    def q_out(pair, n):
        src, dst = ((q_hbm, qin), (g_hbm, gin))[n]
        for k in (1, 3, 2):
            for u in pair:
                t = u % 2
                a, dev = a_peer(t, k)
                remote(
                    src.at[0, pl.ds(first_round(u), PART), :, lanes_of(a, GROUP * DIM)],
                    dst.at[u, me_a(t)], q_send.at[n], q_recv.at[u, n], dev,
                )

    first, second = (0, 1), (2, 3)
    for h in range(HEADS):
        for n, src in enumerate((k_hbm, v_hbm)):
            local(src.at[0, :, :, pl.ds(h * DIM, DIM)], kst.at[n, h], kst_sem)
    pl.semaphore_wait(barrier, 6 + dp)
    drain(kst, kst_sem)
    kv_first(first)
    kv_first(second)
    q_out(first, 0)
    for i in range(1, 8):

        @pl.when(dp >= i)
        def _():
            pl.semaphore_signal(hello, inc=1, device_id=(dp - i, ctx), device_id_type=MESH)

    local(gain_hbm, gain_ref, small.at[0])
    local(docs_hbm, docs_ref, small.at[1])
    for u in range(4):
        kv_local(u)
    for u in range(4):
        q_local(u)
    kv_near(first)
    kv_near(second)
    q_out(first, 1)
    kv_far(first)
    q_out(second, 0)
    kv_far(second)
    q_out(second, 1)

    drain(gain_ref, small.at[0])
    drain(docs_ref, small.at[1])
    for i in range(HEADS * GROUP):
        gains[i : i + 1, :] = gain_ref[pl.ds(i * DIM, DIM)].astype(F32).reshape(1, DIM)
    key_i = lax.broadcasted_iota(jnp.int32, (TOK, ROWS), 0)
    row_i = lax.broadcasted_iota(jnp.int32, (TOK, ROWS), 1) & (SIDE * WIDE - 1)
    for t in range(2):
        a_step = WIDE * over_x(t) + WIDE * SIDE * (1 - over_x(t))
        g_step = WIDE * (1 + SIDE) - a_step

        def key_col(i):
            return ((i >> 3) & 3) * a_step + (i >> 5) * g_step + (i & 7)

        def row_col(i):
            return ((i >> 3) & 3) * a_step + me_g(t) * g_step + (i & 7)

        le = key_col(key_i) <= row_col(row_i)
        le_ref[t] = jnp.where(le, 1.0, 0.0)
        perm = jnp.where(
            key_col(lax.broadcasted_iota(jnp.int32, (TOK, TOK), 0)) == lax.broadcasted_iota(jnp.int32, (TOK, TOK), 1),
            1.0, 0.0,
        ).astype(BF16)
        sel = jnp.where(
            row_col(lax.broadcasted_iota(jnp.int32, (ROWS, TOK), 0)) == lax.broadcasted_iota(jnp.int32, (ROWS, TOK), 1),
            1.0, 0.0,
        ).astype(BF16)

        def doc_row(r):
            return docs_ref[0:1, pl.ds(pl.multiple_of(r * TOK, TOK), TOK)].astype(F32)

        def one_bias(r, _):
            rho = 2 * PART * t + r
            cur = doc_row(rho)
            prev = doc_row((rho + ROUNDS - 1) % ROUNDS)
            k_cur = dot_t(perm, jnp.broadcast_to(cur, (ROWS, TOK)).astype(BF16))
            k_prev = dot_t(perm, jnp.broadcast_to(prev, (ROWS, TOK)).astype(BF16))
            q_doc = dot_t(jnp.broadcast_to(cur, (TOK, TOK)).astype(BF16), sel)
            k_prev = jnp.where(rho > 0, k_prev, -1.0)
            mine = jnp.where(le_ref[t] > 0.5, k_cur, k_prev)
            bias_ref[t, r] = jnp.where(mine == q_doc, 0.0, NEG_BIG)
            return 0

        lax.fori_loop(0, 2 * PART, one_bias, 0)

    def bulk(pair, r, count):
        for n, (buf, dst) in enumerate(((att_o, att_hbm), (dq_o, dq_hbm))):
            for k in (1, 3, 2, 0):
                for u in pair:
                    t = u % 2
                    there = dst.at[0, pl.ds(first_round(u) + r, count), :, lanes_of(me_a(t), GROUP * DIM)]
                    b, dev = a_peer(t, k)
                    here = buf.at[u, b, pl.ds(r, count)]
                    if k:
                        remote(here, there, out_send.at[n], out_recv.at[n], dev)
                    else:
                        local(here, there, out_recv.at[n])

    def compute(pair):
        for u in pair:
            slots = key_rounds(u)[1]
            for n, buf in enumerate((qin, gin)):
                drain(buf.at[u], q_recv.at[u, n])
            for n, (buf, rest) in enumerate(((kin, (2, 3)), (vin, (1, 2)))):
                for k in rest:
                    drain(buf.at[u % 2, 0, :, slots], kvg_recv.at[u, n, k - 1])

        def one_round(u, r):
            t = u % 2
            h = me_a(t)
            here = PART * (u // 2) + r + t
            before = here - ((r + PART - 1) // PART if u == 0 else 1)

            def gain_row(g):
                return gains[pl.ds(h * GROUP + g, 1), :]

            def keys(buf, s):
                return buf[t, :, :, s].astype(F32).reshape(TOK, DIM)

            k_win = jnp.concatenate([keys(kin, here), keys(kin, before)], axis=0).astype(BF16)
            v_win = jnp.concatenate([keys(vin, here), keys(vin, before)], axis=0).astype(BF16)
            q_rows = jnp.concatenate(
                [qin[u, :, r, :, g * DIM : (g + 1) * DIM].astype(F32).reshape(SIDE * WIDE, DIM) for g in range(GROUP)],
                axis=0,
            ).astype(BF16)
            hg = jnp.concatenate(
                [
                    gin[u, :, r, :, g * DIM : (g + 1) * DIM].astype(F32).reshape(SIDE * WIDE, DIM)
                    * gain_row(g)
                    for g in range(GROUP)
                ],
                axis=0,
            ).astype(BF16)
            le = le_ref[t] > 0.5
            s_all = dot_t(k_win, q_rows)
            s = jnp.where(le, s_all[:TOK], s_all[TOK:]) * (scale * math.log2(math.e)) + bias_ref[t, PART * (u // 2) + r]
            e = jnp.exp2(s - jnp.max(s, axis=0, keepdims=True))
            p = e * (1.0 / jnp.sum(e, axis=0, keepdims=True))
            d_all = dot_t(v_win, hg)
            d = jnp.where(le, d_all[:TOK], d_all[TOK:])
            ds = p * (d - jnp.sum(p * d, axis=0, keepdims=True))
            p2 = jnp.concatenate([jnp.where(le, p, 0.0), jnp.where(le, 0.0, p)], axis=0).astype(BF16)
            ds2 = jnp.concatenate([jnp.where(le, ds, 0.0), jnp.where(le, 0.0, ds)], axis=0).astype(BF16)
            attn = dot_tn(p2, v_win).astype(BF16).astype(F32)
            dq = dot_tn(ds2, k_win) * scale
            dv = dot_n(p2, hg)
            dk = dot_n(ds2, q_rows) * scale
            for g in range(GROUP):
                rows = slice(g * SIDE * WIDE, (g + 1) * SIDE * WIDE)
                cols = slice(g * DIM, (g + 1) * DIM)
                a_g = attn[rows].reshape(SIDE, WIDE, DIM)
                gacc[t, g] += jnp.sum(a_g * gin[u, :, r, :, cols].astype(F32), axis=0)
                att_o[u, :, r, :, cols] = (a_g * gain_row(g)).astype(BF16)
                dq_o[u, :, r, :, cols] = dq[rows].reshape(SIDE, WIDE, DIM).astype(BF16)
            kp[t, :, :, before] = (kacc[t] + dk[TOK:]).reshape(SIDE, SIDE, WIDE, DIM).astype(BF16)
            vp[t, :, :, before] = (vacc[t] + dv[TOK:]).reshape(SIDE, SIDE, WIDE, DIM).astype(BF16)
            kacc[t] = dk[:TOK]
            vacc[t] = dv[:TOK]

        def both(r, _):
            for u in pair:
                one_round(u, r)
            return 0

        lax.fori_loop(0, PART, both, 0)

    def end_of_rounds():
        for t in range(2):
            last = 2 * PART - 1 + t
            kp[t, :, :, last] = kacc[t].reshape(SIDE, SIDE, WIDE, DIM).astype(BF16)
            vp[t, :, :, last] = vacc[t].reshape(SIDE, SIDE, WIDE, DIM).astype(BF16)
            for g in range(GROUP):
                gpart[t, g // 2, g % 2 : g % 2 + 1, :] = jnp.sum(gacc[t, g], axis=0, keepdims=True)

    def grad_slots(u):
        return pl.ds(*OUT_SLOTS[u])

    def sums_near(pair):
        for n, (part, got, k) in enumerate(((kp, kr, 3), (vp, vr, 1))):
            for u in pair:
                t, slots = u % 2, grad_slots(u)
                remote(
                    part.at[t, (me_g(t) + 2) % SIDE, :, slots], got.at[t, 1, :, slots],
                    rs_send.at[u, n], rs_recv.at[u, n, 1], g_peer(t, SIDE - k)[1],
                )
        for n, (part, got, k) in enumerate(((kp, kr, 3), (vp, vr, 1))):
            for u in pair:
                t, slots = u % 2, grad_slots(u)
                g, dev = g_peer(t, k)
                remote(
                    part.at[t, g, :, slots], got.at[t, 0, :, slots], rs_send.at[u, n], rs_recv.at[u, n, 0], dev
                )

    def sums_far(pair):
        for n, (part, got, k) in enumerate(((kp, kr, 1), (vp, vr, 3))):
            for u in pair:
                t, slots = u % 2, grad_slots(u)
                g, dev = g_peer(t, k)
                drain(got.at[t, 1, :, slots], rs_recv.at[u, n, 1])
                got[t, 1, :, slots] = (
                    got[t, 1, :, slots].astype(F32) + part[t, g, :, slots].astype(F32)
                ).astype(BF16)
                remote(
                    got.at[t, 1, :, slots], got.at[t, 2, :, slots], rs_send.at[u, n], rs_recv.at[u, n, 2], dev
                )

    def sums_back(pair):
        for n, (part, got, total, back) in enumerate(((kp, kr, ks, ka), (vp, vr, vs, va))):
            for u in pair:
                t, slots = u % 2, grad_slots(u)
                drain(got.at[t, 0, :, slots], rs_recv.at[u, n, 0])
                drain(got.at[t, 2, :, slots], rs_recv.at[u, n, 2])
                total[t, :, slots] = (
                    part[t, me_g(t), :, slots].astype(F32)
                    + got[t, 0, :, slots].astype(F32)
                    + got[t, 2, :, slots].astype(F32)
                ).astype(BF16)
            for k in (1, 3, 2):
                for u in pair:
                    t, slots = u % 2, grad_slots(u)
                    b, dev = a_peer(t, k)
                    remote(
                        total.at[t, b, slots], back.at[t, me_a(t), slots], aa_send.at[u, n], aa_recv.at[u, n], dev
                    )
            for u in pair:
                t, slots = u % 2, grad_slots(u)
                local(total.at[t, me_a(t), slots], back.at[t, me_a(t), slots], aa_recv.at[u, n])

    def gain_rows(go):
        @pl.when(z != x)
        def _():
            copy = pltpu.make_async_remote_copy(
                src_ref=gpart.at[core], dst_ref=ghalf.at[(z - x + 3) % SIDE], send_sem=gr_send.at[0],
                recv_sem=gr_recv.at[0], device_id=at_ctx(x * SIDE + x), device_id_type=MESH,
            )
            copy.start() if go else copy.wait_send()

        if go:
            for k in (1, 3, 2):
                i, dev = x_peer(k)
                remote(gpart.at[1 - core, i], gside.at[k - 1], gr_send.at[1], gr_recv.at[1], dev)
        else:
            drain(gpart.at[1, pl.ds(0, SIDE - 1)], gr_send.at[1])

    def gain_cols(go):
        @pl.when(z == x)
        def _():
            if go:
                drain(ghalf, gr_recv.at[0])
                gsum[...] = gpart[core] + ghalf[0] + ghalf[1] + ghalf[2]
                for k in (1, 3, 2):
                    i, dev = x_peer(k)
                    remote(gsum.at[i], gdiag, ga_send, ga_recv, dev)
                gdiag[...] = gsum[x]
            else:
                drain(gsum.at[pl.ds(0, SIDE - 1)], ga_send)

    def gain_over_dp():
        drain(gside, gr_recv.at[1])

        @pl.when(z != x)
        def _():
            drain(gdiag, ga_recv)

        gfin[...] = gdiag[...] + gpart[1 - core, x] + gside[0] + gside[1] + gside[2]
        for i in range(1, 8):
            remote(gfin, gdp.at[i - 1], d_send, d_recv, ((dp + i) % 8, ctx))

    def finish(pair):
        for n, (back, out) in enumerate(((ka, dk_ref), (va, dv_ref))):
            for u in pair:
                t = u % 2
                drain(back.at[t, :, grad_slots(u)], aa_recv.at[u, n])
            for u in pair:
                t = u % 2
                start, count = OUT_SLOTS[u]
                for slot in range(start, start + count):
                    rho = slot + (2 * PART - 1) * t
                    if t == 1 and slot == 0:
                        continue
                    for h in range(HEADS):
                        val = back[t, h, slot]
                        if t == 0 and slot == 2 * PART - 1:
                            val = (val.astype(F32) + back[1, h, 0].astype(F32)).astype(BF16)
                        out[0, rho, :, h * DIM : (h + 1) * DIM] = val

    kacc[...] = jnp.zeros_like(kacc)
    vacc[...] = jnp.zeros_like(vacc)
    gacc[...] = jnp.zeros_like(gacc)
    compute(first)
    sums_near(first)
    bulk(first, 0, PART)
    compute(second)
    end_of_rounds()
    gain_rows(True)
    sums_near(second)
    sums_far(first)
    gain_cols(True)
    bulk(second, 0, 1)
    sums_far(second)
    sums_back(first)

    @pl.when(dp < 7)
    def _():
        pl.semaphore_wait(hello, 7 - dp)

    gain_over_dp()
    bulk(second, 1, 1)
    sums_back(second)
    bulk(second, 2, 2)
    finish(first)
    finish(second)
    drain(gdp, d_recv)
    total = gfin[...]
    for i in range(7):
        total += gdp[i]
    for i in range(2):
        gg_ref[pl.ds(i * DIM, DIM)] = total[i] * (1.0 / 128.0)
    for u in range(4):
        t, slots, grads = u % 2, key_rounds(u)[1], grad_slots(u)
        for n, buf in enumerate((kin, vin)):
            drain(buf.at[t, 0, pl.ds(0, SIDE - 1), slots], kv_send.at[u, n])
            drain(buf.at[t, pl.ds(0, SIDE - 1), :, slots], kvg_send.at[u, n])
        for n, (got, back) in enumerate(((kr, ka), (vr, va))):
            drain(got.at[t, :, :, grads], rs_send.at[u, n])
            drain(back.at[t, pl.ds(0, SIDE - 1), grads], aa_send.at[u, n])
    for n, buf in enumerate((qin, gin)):
        drain(buf.at[:, pl.ds(0, SIDE - 1)], q_send.at[n])
    for n, (buf, dst) in enumerate(((att_o, att_hbm), (dq_o, dq_hbm))):
        drain(buf.at[:, pl.ds(0, SIDE - 1)], out_send.at[n])
        drain(dst, out_recv.at[n])
    gain_rows(False)
    gain_cols(False)
    drain(gdp, d_send)


def write_out(att, dq, dk, dv, gg, att_out, dq_out, dk_out, dv_out, gg_out, big, small):
    copies = []
    for n, (src, dst) in enumerate(((att, att_out), (dq, dq_out))):
        for i in range(4):
            part = pl.ds(i * 4, 4)
            copies.append(pltpu.make_async_copy(src.at[:, part], dst.at[:, part], big.at[n, i]))
    for n, (src, dst) in enumerate(((dk, dk_out), (dv, dv_out), (gg, gg_out))):
        copies.append(pltpu.make_async_copy(src, dst, small.at[n]))
    for copy in copies:
        copy.start()
    for copy in copies:
        copy.wait()


def body(queries, key_rows, values, out_grad, out_gain, documents):
    queries, key_rows, values, out_grad, out_gain, documents = (
        pltpu.with_memory_space_constraint(a, pltpu.HBM)
        for a in (queries, key_rows, values, out_grad, out_gain, documents)
    )
    any_spec = pl.BlockSpec(memory_space=pl.ANY)
    vmem = pl.BlockSpec(memory_space=pltpu.VMEM)
    wide = pltpu.VMEM((4, SIDE, PART, WIDE, GROUP * DIM), BF16)
    narrow = pltpu.VMEM((2, SIDE, SIDE, SLOTS, WIDE, DIM), BF16)
    narrow3 = pltpu.VMEM((2, SIDE - 1, SIDE, SLOTS, WIDE, DIM), BF16)
    flat = pltpu.VMEM((2, SIDE, SLOTS, WIDE, DIM), BF16)
    dma = pltpu.SemaphoreType.DMA
    att, dq, dk, dv, gg = pl.pallas_call(
        kernel,
        out_shape=(
            jax.ShapeDtypeStruct(queries.shape, BF16),
            jax.ShapeDtypeStruct(queries.shape, BF16),
            jax.ShapeDtypeStruct(key_rows.shape, BF16),
            jax.ShapeDtypeStruct(key_rows.shape, BF16),
            jax.ShapeDtypeStruct((2 * DIM,), F32),
        ),
        in_specs=[any_spec] * 6,
        out_specs=(any_spec, any_spec, vmem, vmem, vmem),
        scratch_shapes=[
            wide, wide, narrow, narrow, wide, wide, narrow, narrow, narrow3, narrow3, flat, flat, flat, flat,
            pltpu.VMEM((2, 4, ROUNDS, WIDE, DIM), BF16),
            pltpu.VMEM(out_gain.shape, BF16),
            pltpu.VMEM(documents.shape, jnp.int32),
            pltpu.VMEM((2, TOK, ROWS), F32),
            pltpu.VMEM((2, 2 * PART, TOK, ROWS), F32),
            pltpu.VMEM((2, TOK, DIM), F32),
            pltpu.VMEM((2, TOK, DIM), F32),
            pltpu.VMEM((2, GROUP, WIDE, DIM), F32),
            pltpu.VMEM((HEADS * GROUP, DIM), F32),
            pltpu.VMEM((2, SIDE, 2, DIM), F32),
            pltpu.VMEM((SIDE - 1, SIDE, 2, DIM), F32),
            pltpu.VMEM((SIDE, 2, DIM), F32),
            pltpu.VMEM((SIDE - 1, 2, DIM), F32),
            pltpu.VMEM((2, DIM), F32),
            pltpu.VMEM((2, DIM), F32),
            pltpu.VMEM((7, 2, DIM), F32),
            dma((4, 2)), dma((4, 2)), dma((4, 2)), dma((4, 2, 3)), dma((2,)), dma((4, 2)), dma((2,)), dma((2,)),
            dma((4, 2)), dma((4, 2, 3)), dma((4, 2)), dma((4, 2)), dma((2,)), dma((2,)), dma, dma, dma, dma,
            dma((2,)), pltpu.SemaphoreType.REGULAR, dma,
        ],
        compiler_params=pltpu.CompilerParams(
            collective_id=0, has_side_effects=True, vmem_limit_bytes=48 * 1024 * 1024
        ),
        name="packed_attention",
    )(queries, key_rows, values, out_grad, out_gain, documents)
    return pl.pallas_call(
        write_out,
        out_shape=(
            jax.ShapeDtypeStruct(queries.shape, BF16),
            jax.ShapeDtypeStruct(queries.shape, BF16),
            jax.ShapeDtypeStruct(key_rows.shape, BF16),
            jax.ShapeDtypeStruct(key_rows.shape, BF16),
            jax.ShapeDtypeStruct((2 * DIM,), F32),
        ),
        in_specs=[any_spec] * 5,
        out_specs=(any_spec,) * 5,
        scratch_shapes=[dma((2, 4)), dma((3,))],
        compiler_params=pltpu.CompilerParams(vmem_limit_bytes=1024 * 1024),
        name="write_out",
    )(att, dq, dk, dv, gg)


def solution(mesh):
    tokens = P("dp", None, "ctx", None)
    return jax.shard_map(
        body,
        mesh=mesh,
        in_specs=(tokens, tokens, tokens, tokens, P(), P("dp", None)),
        out_specs=(tokens, tokens, tokens, tokens, P("ctx")),
        check_vma=False,
    )
```
